32 devices in a mesh: groups: 2 (over y), seq: 4 (over z), tp: 4 (over x, core).
Axes of the slice: x: 2, y: 2, z: 4, core: 2. Of those that a mesh axis runs over, the one named last changes fastest.
Arguments:
- query: bfloat16 [4096, 2048], P(('groups', 'seq'), 'tp'), parts along dimension 0, may hold values from -64 to 64
- key_head_rows: bfloat16 [4096, 512], P(('groups', 'seq'), 'tp'), parts along dimension 0, may hold values from -64 to 64
- value_head_rows: bfloat16 [4096, 512], P(('groups', 'seq'), 'tp'), parts along dimension 0, may hold values from -6 to 6
- output_gradient: bfloat16 [4096, 2048], P(('groups', 'seq'), 'tp'), parts along dimension 0, may hold values from -16 to 16
- doc_blocks: int32 [32, 8], P(('groups', 'seq')), parts along dimension 0, may hold values from 0 to 13, as said below
- w_query: bfloat16 [4096, 2048], P(None, 'tp'), may hold values from -0.5 to 0.5
- key_weight: bfloat16 [4096, 512], P(None, 'tp'), may hold values from -0.5 to 0.5
- value_weight: bfloat16 [4096, 512], P(None, 'tp'), may hold values from -0.5 to 0.5
Outputs:
- input_grad: bfloat16 [4096, 4096], P(('groups', 'seq'), 'tp'), parts along dimension 0
The draws below stay inside these ranges and needn't reach their ends.
There are 2 independent parts, one for each index of `groups`. The reference program is written for one: setup_inputs(seed, part) draws one part's arguments, and reference() takes and returns one part's arrays. A program takes and returns all parts, laid end to end along the dimension named above; an argument that names none is the same for every part. Nothing has to cross between parts.
Inputs may be any that keep to these rules, and one draw needn't show every extreme that they name: `doc_blocks`: row b holds max(b - o, 0) for 8 distinct offsets o of 2 to 12; every row b that starts a shard of 512 positions uses the offset 12, and the last row uses the offset 2.
All inputs are finite; a program needn't handle non-finite values.
Results may differ from the reference program's by a relative error of at most 0.014.
Values may be sent and summed in bfloat16 or wider, within the bound.
No kernel may reach another device: no remote copies, remote signals or barrier semaphores. Data moves between devices by JAX's collectives and lax.ppermute only.
A program may use at most 128 MiB of HBM per device.

```python
import jax
import jax.numpy as jnp
from jax import lax

MODEL_WIDTH = 4096
QUERY_HEADS = 16
KEY_VALUE_HEADS = 4
HEAD_WIDTH = 128
BLOCK_POSITIONS = 128
LISTED_COUNT = 8
TOK_DEV = 512
TOKEN_COUNT = 2048
QUERY_BLOCK_COUNT = 16
SPAN_BLK = 12
N_TP = 4


def paired_rows(key):
    query_raw = jnp.clip(jax.random.normal(jax.random.fold_in(key, 11), (TOKEN_COUNT, QUERY_HEADS * HEAD_WIDTH), jnp.float32), -6.0, 6.0)
    key_unprojected = jnp.clip(jax.random.normal(jax.random.fold_in(key, 12), (TOKEN_COUNT, KEY_VALUE_HEADS * HEAD_WIDTH), jnp.float32), -6.0, 6.0)
    return (query_raw, key_unprojected)


def draw_query(key, part):
    return paired_rows(key)[0].astype(jnp.bfloat16)


def draw_key_head_rows(key, part):
    return paired_rows(key)[1].astype(jnp.bfloat16)


def draw_doc_blocks(key, part):
    option_count = SPAN_BLK - 1
    raw_scores = jax.random.randint(key, (QUERY_BLOCK_COUNT, option_count), 0, 1 << 20)
    sorted_scores = raw_scores * SPAN_BLK + jnp.arange(option_count)[None, :]
    row_index = jnp.arange(QUERY_BLOCK_COUNT)
    column_number = jnp.arange(option_count)[None, :]
    foremost_entries = row_index % (TOK_DEV // BLOCK_POSITIONS) == 0
    extra_score = jnp.where(foremost_entries[:, None] & (column_number == option_count - 1), 1 << 30, 0)
    closing_row = row_index == QUERY_BLOCK_COUNT - 1
    extra_score = extra_score + jnp.where(closing_row[:, None] & (column_number == 0), 1 << 30, 0)
    highest_values, selected_blocks = lax.top_k(sorted_scores + extra_score, LISTED_COUNT)
    block_ids = row_index[:, None] - (selected_blocks + 2)
    return jnp.maximum(block_ids, 0).astype(jnp.int32)


def level_of(key, extent, shards, smallest, largest):
    loudness = 1.0
    for dim, blocks in shards:
        steps = jax.random.uniform(jax.random.fold_in(jax.random.fold_in(key, 6), dim), (blocks,), jnp.float32, smallest / len(shards), largest / len(shards))
        loudness = loudness * jnp.repeat(jnp.exp(steps), extent[dim] // blocks).reshape((-1,) + (1,) * (len(extent) - 1 - dim))
    return loudness


def centred(own_key, shape, scale, limit, pieces=(), kind=jnp.bfloat16):
    level = level_of(own_key, shape, pieces, -0.22, 0.18) if pieces else 1.0
    result = jax.random.normal(own_key, shape, jnp.float32) * scale * level
    return jnp.minimum(jnp.maximum(result, -limit), limit).astype(kind)


def setup_inputs(seed: int = 0, part: int = 0) -> dict:
    splits = jax.random.split(jax.random.key(seed), 9)
    part_keys = jax.random.split(jax.random.fold_in(splits[8], part), 9)
    query = draw_query(jax.random.fold_in(jax.random.fold_in(splits[8], part), 71), part)
    key_head_rows = draw_key_head_rows(jax.random.fold_in(jax.random.fold_in(splits[8], part), 71), part)
    value_head_rows = centred(part_keys[2], (TOKEN_COUNT, KEY_VALUE_HEADS * HEAD_WIDTH), 1.0, 6.0, ((0, 4), (1, 4)))
    output_gradient = centred(part_keys[3], (TOKEN_COUNT, QUERY_HEADS * HEAD_WIDTH), 4.0, 16.0, ((0, 4), (1, 4)))
    doc_blocks = draw_doc_blocks(jax.random.fold_in(jax.random.fold_in(splits[8], part), 71), part)
    w_query = centred(splits[5], (MODEL_WIDTH, QUERY_HEADS * HEAD_WIDTH), HEAD_WIDTH ** -0.5, 0.5, ((1, 4),))
    key_weight = centred(splits[6], (MODEL_WIDTH, KEY_VALUE_HEADS * HEAD_WIDTH), HEAD_WIDTH ** -0.5, 0.5, ((1, 4),))
    value_weight = centred(splits[7], (MODEL_WIDTH, KEY_VALUE_HEADS * HEAD_WIDTH), HEAD_WIDTH ** -0.5, 0.5, ((1, 4),))
    return dict(query=query, key_head_rows=key_head_rows, value_head_rows=value_head_rows, output_gradient=output_gradient, doc_blocks=doc_blocks, w_query=w_query, key_weight=key_weight, value_weight=value_weight)


def block_grads(query_block, grad_block, key_block, value_block, allowed):
    score_scale = HEAD_WIDTH ** -0.5
    query_full = query_block.astype(jnp.float32)
    grad_full = grad_block.astype(jnp.float32)
    key_full = key_block.astype(jnp.float32)
    value_full = value_block.astype(jnp.float32)
    scores = jnp.einsum("qhgd,khd->hgqk", query_full, key_full) * score_scale
    scores = jnp.where(allowed, scores, -jnp.inf)
    row_max = jnp.max(scores, axis=-1, keepdims=True)
    weights = jnp.where(allowed, jnp.exp(scores - row_max), 0.0)
    probability = weights / jnp.sum(weights, axis=-1, keepdims=True)
    prob_half = lax.optimization_barrier(probability.astype(jnp.bfloat16)).astype(jnp.float32)
    attended = jnp.einsum("hgqk,khd->qhgd", prob_half, value_full)
    row_delta = jnp.sum(grad_full * attended, axis=-1)
    prob_grad = jnp.einsum("qhgd,khd->hgqk", grad_full, value_full)
    score_grad = probability * (prob_grad - jnp.transpose(row_delta, (1, 2, 0))[..., None])
    score_half = lax.optimization_barrier(score_grad.astype(jnp.bfloat16)).astype(jnp.float32)
    query_grad = jnp.einsum("hgqk,khd->qhgd", score_half, key_full) * score_scale
    key_gradient = jnp.einsum("hgqk,qhgd->khd", score_half, query_full) * score_scale
    value_gradient = jnp.einsum("hgqk,qhgd->khd", prob_half, grad_full)
    return query_grad, key_gradient, value_gradient


def reference(query, key_head_rows, value_head_rows, output_gradient, doc_blocks, w_query, key_weight, value_weight):
    group_width = QUERY_HEADS // KEY_VALUE_HEADS
    listed_slot_count = LISTED_COUNT + 2
    query_block_rows = query.reshape(QUERY_BLOCK_COUNT, BLOCK_POSITIONS, KEY_VALUE_HEADS, group_width, HEAD_WIDTH)
    gradient_blocks = output_gradient.reshape(QUERY_BLOCK_COUNT, BLOCK_POSITIONS, KEY_VALUE_HEADS, group_width, HEAD_WIDTH)
    key_block_rows = key_head_rows.reshape(QUERY_BLOCK_COUNT, BLOCK_POSITIONS, KEY_VALUE_HEADS, HEAD_WIDTH)
    value_block_rows = value_head_rows.reshape(QUERY_BLOCK_COUNT, BLOCK_POSITIONS, KEY_VALUE_HEADS, HEAD_WIDTH)
    offsets = jnp.arange(BLOCK_POSITIONS, dtype=jnp.int32)
    earlier = jnp.arange(LISTED_COUNT)[:, None] > jnp.arange(LISTED_COUNT)[None, :]
    far_slot = jnp.repeat(jnp.arange(listed_slot_count) >= 2, BLOCK_POSITIONS)

    def visit_block(sums_carry, block_id):
        key_gradient_sum, value_gradient_sum = sums_carry
        listed = doc_blocks[block_id].astype(jnp.int32)
        repeated = jnp.any((listed[:, None] == listed[None, :]) & earlier, axis=1)
        listed_ok = (listed <= block_id - 2) & jnp.logical_not(repeated)
        band_ids = jnp.stack([block_id - 1, block_id]).astype(jnp.int32)
        slot_ids = jnp.concatenate([band_ids, listed])
        slot_ok = jnp.concatenate([jnp.stack([block_id >= 1, block_id >= 0]), listed_ok])
        clamped_index = jnp.maximum(slot_ids, 0)
        query_pos = block_id * BLOCK_POSITIONS + offsets
        key_pos = (slot_ids[:, None] * BLOCK_POSITIONS + offsets[None, :]).reshape(-1)
        in_reach = (key_pos[None, :] <= query_pos[:, None]) & (query_pos[:, None] - key_pos[None, :] < BLOCK_POSITIONS)
        allowed = jnp.repeat(slot_ok, BLOCK_POSITIONS)[None, :] & (far_slot[None, :] | in_reach)
        present_keys = key_block_rows[clamped_index].reshape(listed_slot_count * BLOCK_POSITIONS, KEY_VALUE_HEADS, HEAD_WIDTH)
        present_values = value_block_rows[clamped_index].reshape(listed_slot_count * BLOCK_POSITIONS, KEY_VALUE_HEADS, HEAD_WIDTH)
        query_grad, key_gradient, value_gradient = block_grads(query_block_rows[block_id], gradient_blocks[block_id], present_keys, present_values, allowed)
        key_gradient_sum = key_gradient_sum.at[clamped_index].add(key_gradient.reshape(listed_slot_count, BLOCK_POSITIONS, KEY_VALUE_HEADS, HEAD_WIDTH))
        value_gradient_sum = value_gradient_sum.at[clamped_index].add(value_gradient.reshape(listed_slot_count, BLOCK_POSITIONS, KEY_VALUE_HEADS, HEAD_WIDTH))
        return (key_gradient_sum, value_gradient_sum), query_grad.astype(jnp.bfloat16)

    initial_zeros = jnp.zeros((QUERY_BLOCK_COUNT, BLOCK_POSITIONS, KEY_VALUE_HEADS, HEAD_WIDTH), jnp.float32)
    closing_sums, query_grads = lax.scan(visit_block, (initial_zeros, initial_zeros), jnp.arange(QUERY_BLOCK_COUNT, dtype=jnp.int32))
    query_grad_all = query_grads.reshape(TOKEN_COUNT, QUERY_HEADS * HEAD_WIDTH)
    key_gradient_total = closing_sums[0].reshape(TOKEN_COUNT, KEY_VALUE_HEADS * HEAD_WIDTH).astype(jnp.bfloat16)
    value_gradient_total = closing_sums[1].reshape(TOKEN_COUNT, KEY_VALUE_HEADS * HEAD_WIDTH).astype(jnp.bfloat16)
    query_cols = QUERY_HEADS * HEAD_WIDTH // N_TP
    key_value_columns = KEY_VALUE_HEADS * HEAD_WIDTH // N_TP
    summed = jnp.zeros((TOKEN_COUNT, MODEL_WIDTH), jnp.float32)
    for shard_index in range(N_TP):
        query_span = slice(shard_index * query_cols, (shard_index + 1) * query_cols)
        kv_span = slice(shard_index * key_value_columns, (shard_index + 1) * key_value_columns)
        grad_term = jnp.dot(query_grad_all[:, query_span], w_query[:, query_span].T, preferred_element_type=jnp.float32)
        grad_term = grad_term + jnp.dot(key_gradient_total[:, kv_span], key_weight[:, kv_span].T, preferred_element_type=jnp.float32)
        grad_term = grad_term + jnp.dot(value_gradient_total[:, kv_span], value_weight[:, kv_span].T, preferred_element_type=jnp.float32)
        summed = summed + lax.optimization_barrier(grad_term.astype(jnp.bfloat16)).astype(jnp.float32)
    return summed.astype(jnp.bfloat16)
```

```python
import functools

import jax
import jax.numpy as jnp
from jax import lax
from jax.experimental import pallas as pl
from jax.experimental.pallas import tpu as pltpu
from jax.sharding import PartitionSpec as P

HEAD_WIDTH = 128
BLOCK = 128
SCALE = HEAD_WIDTH ** (-0.5)
SCALE_LOG2 = SCALE * 1.4426950408889634
LOWEST = -1e30
NT = (((1,), (1,)), ((), ()))


def shifted(block, axis, distance):
    devices = range(lax.axis_size(axis))
    route = [(i - distance, i) for i in devices if i - distance in devices]
    return lax.ppermute(block, axis, route)


def swapped(block, axis, bits):
    return lax.ppermute(block, axis, [(i, i ^ bits) for i in range(lax.axis_size(axis))])


def key_range(distance, i, blocks, reach):
    if distance == 0:
        return 0, i + 1
    if distance == reach:
        return i, blocks
    return 0, blocks


def lane_range(distance, j, blocks, reach):
    if distance == 0:
        return j, blocks
    if distance == reach:
        return 0, j + 1
    return 0, blocks


def stack_heads(rows_ref, stack_ref, blocks, heads):
    for i in range(blocks):
        for h in range(heads):
            at = (i * heads + h) * BLOCK
            stack_ref[at : at + BLOCK, :] = rows_ref[
                i * BLOCK : (i + 1) * BLOCK, h * HEAD_WIDTH : (h + 1) * HEAD_WIDTH
            ]


def band_keep(offset, lanes):
    key_at = lax.broadcasted_iota(jnp.int32, (BLOCK, lanes), 0)
    query_at = lax.broadcasted_iota(jnp.int32, (BLOCK, lanes), 1) % BLOCK
    return key_at <= query_at if offset == 0 else key_at > query_at


def fold(tile, op):
    rows = tile.shape[0]
    total = tile[0:8]
    for at in range(8, rows, 8):
        total = op(total, tile[at : at + 8])
    return total


def tiles_of(distances, i, blocks, reach):
    return [
        (c, d, j)
        for c, d in enumerate(distances)
        for j in range(*key_range(d, i, blocks, reach))
    ]


def score_pass(i, distances, blocks, reach, flag_ref, key_refs, value_refs, query_i, grad_i, s_ref, g_ref):
    rows = blocks * BLOCK
    top = None
    for c, d in enumerate(distances):
        low, high = key_range(d, i, blocks, reach)
        span = slice(low * BLOCK, high * BLOCK)
        at = slice(c * rows + low * BLOCK, c * rows + high * BLOCK)
        s_ref[at, :] = lax.dot_general(key_refs[c][span, :], query_i, NT, preferred_element_type=jnp.float32)
        g_ref[at, :] = lax.dot_general(value_refs[c][span, :], grad_i, NT, preferred_element_type=jnp.float32)
    for c, d, j in tiles_of(distances, i, blocks, reach):
        at = slice(c * rows + j * BLOCK, c * rows + (j + 1) * BLOCK)
        offset = d * blocks + i - j
        tile = s_ref[at, :]
        if offset < 2:
            tile = jnp.where(band_keep(offset, tile.shape[1]), tile, LOWEST)
            s_ref[at, :] = tile
        part = fold(tile, jnp.maximum)
        if offset > 0:
            part = jnp.where(flag_ref[i, d * blocks + j] != 0, part, LOWEST)
        top = part if top is None else jnp.maximum(top, part)
    return jnp.max(top, axis=0, keepdims=True)


def shift_of(flag_ref, i, d, j, blocks, base):
    if d * blocks + i - j == 0:
        return base
    return jnp.where(flag_ref[i, d * blocks + j] != 0, base, -LOWEST)


def weight_pass(i, distances, blocks, reach, flag_ref, s_ref, g_ref, base, keep):
    rows = blocks * BLOCK
    total = dot_total = None
    for c, d, j in tiles_of(distances, i, blocks, reach):
        at = slice(c * rows + j * BLOCK, c * rows + (j + 1) * BLOCK)
        weights = jnp.exp2(s_ref[at, :] * SCALE_LOG2 - shift_of(flag_ref, i, d, j, blocks, base))
        if keep:
            s_ref[at, :] = weights
        part = fold(weights, jnp.add)
        dot_part = fold(weights * g_ref[at, :], jnp.add)
        total = part if total is None else total + part
        dot_total = dot_part if dot_total is None else dot_total + dot_part
    return jnp.sum(total, axis=0, keepdims=True), jnp.sum(dot_total, axis=0, keepdims=True)


def key_value_sums(c, d, blocks, reach, lanes, p_ref, ds_ref, query_stack, grad_stack, out_ref):
    rows = blocks * BLOCK
    for j in range(blocks):
        low, high = lane_range(d, j, blocks, reach)
        at = slice(c * rows + j * BLOCK, c * rows + (j + 1) * BLOCK)
        span = slice(low * lanes, high * lanes)
        out = slice(j * BLOCK, (j + 1) * BLOCK)
        key_sum = jnp.dot(ds_ref[at, span], query_stack[span, :], preferred_element_type=jnp.float32)
        out_ref[0, out, :] = (key_sum * SCALE).astype(out_ref.dtype)
        value_sum = jnp.dot(p_ref[at, span], grad_stack[span, :], preferred_element_type=jnp.float32)
        out_ref[1, out, :] = value_sum.astype(out_ref.dtype)


def query_sum(i, distances, blocks, reach, lanes, key_turned, ds_ref):
    rows = blocks * BLOCK
    total = None
    for c, d in enumerate(distances):
        low, high = key_range(d, i, blocks, reach)
        at = slice(c * rows + low * BLOCK, c * rows + high * BLOCK)
        part = jnp.dot(
            key_turned[:, at], ds_ref[at, i * lanes : (i + 1) * lanes], preferred_element_type=jnp.float32
        )
        total = part if total is None else total + part
    return total


def near_stats_kernel(blocks, reach, heads, flag_ref, query_ref, grad_ref, k0, v0, kv1, m_ref, l_ref, r_ref, qs, gs, s_ref, g_ref):
    lanes = heads * BLOCK
    stack_heads(query_ref, qs, blocks, heads)
    stack_heads(grad_ref, gs, blocks, heads)
    for i in range(blocks):
        span = slice(i * lanes, (i + 1) * lanes)
        s_i, g_i = s_ref.at[i % 2], g_ref.at[i % 2]
        top = score_pass(
            i, (0, 1), blocks, reach, flag_ref, (k0, kv1.at[0]), (v0, kv1.at[1]), qs[span, :], gs[span, :], s_i, g_i
        )
        total, dot_total = weight_pass(
            i, (0, 1), blocks, reach, flag_ref, s_i, g_i, top * SCALE_LOG2, False
        )
        m_ref[i : i + 1, :] = top
        l_ref[i : i + 1, :] = total
        r_ref[i : i + 1, :] = dot_total


def gradients(i, distances, blocks, reach, lanes, s_i, g_i, p_ref, ds_ref, inverse, delta):
    rows = blocks * BLOCK
    span = slice(i * lanes, (i + 1) * lanes)
    for c, d, j in tiles_of(distances, i, blocks, reach):
        at = slice(c * rows + j * BLOCK, c * rows + (j + 1) * BLOCK)
        probability = s_i[at, :] * inverse
        p_ref[at, span] = probability.astype(jnp.bfloat16)
        ds_ref[at, span] = (probability * (g_i[at, :] - delta)).astype(jnp.bfloat16)


def far_kernel(blocks, reach, heads, distances, *refs):
    count = len(distances)
    flag_ref, query_ref, grad_ref, m_ref, l_ref, r_ref = refs[:6]
    kv_refs = refs[6 : 6 + count]
    stat_ref, part_ref = refs[6 + count : 8 + count]
    out_refs = refs[8 + count : 8 + 2 * count]
    qs, gs, kt, s_ref, g_ref, p_ref, ds_ref = refs[8 + 2 * count :]
    lanes = heads * BLOCK
    rows = blocks * BLOCK
    stack_heads(query_ref, qs, blocks, heads)
    stack_heads(grad_ref, gs, blocks, heads)
    keys = [r.at[0] for r in kv_refs]
    values = [r.at[1] for r in kv_refs]
    for c in range(count):
        kt[:, c * rows : (c + 1) * rows] = keys[c][...].T
    for i in range(blocks):
        span = slice(i * lanes, (i + 1) * lanes)
        s_i, g_i = s_ref.at[i % 2], g_ref.at[i % 2]
        top = score_pass(
            i, distances, blocks, reach, flag_ref, keys, values, qs[span, :], gs[span, :], s_i, g_i
        )
        before = m_ref[i : i + 1, :]
        top = jnp.maximum(top, before)
        base = top * SCALE_LOG2
        total, dot_total = weight_pass(i, distances, blocks, reach, flag_ref, s_i, g_i, base, True)
        fade = jnp.exp2(before * SCALE_LOG2 - base)
        total = total + l_ref[i : i + 1, :] * fade
        dot_total = dot_total + r_ref[i : i + 1, :] * fade
        inverse = 1.0 / total
        delta = dot_total * inverse
        stat_ref[0, i : i + 1, :] = base
        stat_ref[1, i : i + 1, :] = inverse
        stat_ref[2, i : i + 1, :] = delta
        gradients(i, distances, blocks, reach, lanes, s_i, g_i, p_ref, ds_ref, inverse, delta)
    for c, d in enumerate(distances):
        key_value_sums(c, d, blocks, reach, lanes, p_ref, ds_ref, qs, gs, out_refs[c])
    for i in range(blocks):
        part_ref[i] = query_sum(i, distances, blocks, reach, lanes, kt, ds_ref)


def near_kernel(blocks, reach, heads, far, flag_ref, query_ref, grad_ref, k0, v0, kv1, stat_ref, *refs):
    part_ref, refs = (refs[0], refs[1:]) if far else (None, refs)
    out0_ref, out1_ref, dq_ref, qs, gs, kt, s_ref, g_ref, p_ref, ds_ref = refs
    lanes = heads * BLOCK
    rows = blocks * BLOCK
    distances = (0, 1)
    stack_heads(query_ref, qs, blocks, heads)
    stack_heads(grad_ref, gs, blocks, heads)
    keys, values = (k0, kv1.at[0]), (v0, kv1.at[1])
    for c in range(2):
        kt[:, c * rows : (c + 1) * rows] = keys[c][...].T
    for i in range(blocks):
        span = slice(i * lanes, (i + 1) * lanes)
        s_i, g_i = s_ref.at[i % 2], g_ref.at[i % 2]
        score_pass(
            i, distances, blocks, reach, flag_ref, keys, values, qs[span, :], gs[span, :], s_i, g_i
        )
        base = stat_ref[0, i : i + 1, :]
        weight_pass(i, distances, blocks, reach, flag_ref, s_i, g_i, base, True)
        inverse = stat_ref[1, i : i + 1, :]
        delta = stat_ref[2, i : i + 1, :]
        gradients(i, distances, blocks, reach, lanes, s_i, g_i, p_ref, ds_ref, inverse, delta)
    key_value_sums(1, 1, blocks, reach, lanes, p_ref, ds_ref, qs, gs, out1_ref)
    for i in range(blocks):
        total = query_sum(i, distances, blocks, reach, lanes, kt, ds_ref)
        if far:
            total = total + part_ref[i]
        total = total * SCALE
        for h in range(heads):
            dq_ref[i * BLOCK : (i + 1) * BLOCK, h * HEAD_WIDTH : (h + 1) * HEAD_WIDTH] = (
                total[:, h * BLOCK : (h + 1) * BLOCK].T.astype(dq_ref.dtype)
            )
    key_value_sums(0, 0, blocks, reach, lanes, p_ref, ds_ref, qs, gs, out0_ref)


def kernel_call(kernel, flags, arrays, outs, scratch, flops):
    size = sum(a.size * a.dtype.itemsize for a in arrays) + sum(a.size * a.dtype.itemsize for a in outs)
    held = sum(functools.reduce(lambda a, b: a * b, s.shape) * jnp.dtype(s.dtype).itemsize for s in scratch)
    return pl.pallas_call(
        kernel,
        out_shape=outs,
        in_specs=[pl.BlockSpec(memory_space=pltpu.SMEM)] + [pl.BlockSpec(memory_space=pltpu.VMEM)] * len(arrays),
        out_specs=[pl.BlockSpec(memory_space=pltpu.VMEM)] * len(outs),
        scratch_shapes=scratch,
        compiler_params=pltpu.CompilerParams(vmem_limit_bytes=int(held + 2 * size + (12 << 20))),
        cost_estimate=pl.CostEstimate(flops=flops, bytes_accessed=size, transcendentals=0),
    )(flags, *arrays)


def attention_flags(doc_blocks, blocks, reach, place):
    query_ids = place * blocks + jnp.arange(blocks, dtype=jnp.int32)
    column = jnp.arange((reach + 1) * blocks, dtype=jnp.int32)
    key_ids = (place - column // blocks) * blocks + column % blocks
    behind = query_ids[:, None] - key_ids[None, :]
    listed = jnp.any(doc_blocks[:, :, None] == key_ids[None, None, :], axis=1)
    allowed = (key_ids[None, :] >= 0) & ((behind == 0) | (behind == 1) | ((behind >= 2) & listed))
    return allowed.astype(jnp.int32)


def weight_pieces(w, rows_out, tp_place, group_place, group_count, bits):
    share = rows_out // group_count
    peer = tp_place ^ bits
    return lax.dynamic_slice_in_dim(w, peer * rows_out + group_place * share, share, axis=0)


def gathered_rows(piece, group_count, group_place):
    share = piece.shape[0]
    whole = jnp.zeros((share * group_count, piece.shape[1]), piece.dtype)
    whole = lax.dynamic_update_slice_in_dim(whole, piece, group_place * share, axis=0)
    for step in range(1, group_count):
        route = [(i, (i + step) % group_count) for i in range(group_count)]
        other = lax.ppermute(piece, "groups", route)
        source = lax.rem(group_place - step + group_count, group_count)
        whole = lax.dynamic_update_slice_in_dim(whole, other, source * share, axis=0)
    return whole


def body(query, key_head_rows, value_head_rows, output_gradient, doc_blocks, w_query, key_weight, value_weight):
    rows = query.shape[0]
    blocks = rows // BLOCK
    heads = query.shape[1] // key_head_rows.shape[1]
    lanes = heads * BLOCK
    reach = min(8, lax.axis_size("seq") - 1)
    place = lax.axis_index("seq")
    tp_count = lax.axis_size("tp")
    tp_place = lax.axis_index("tp")
    group_count = lax.axis_size("groups")
    group_place = lax.axis_index("groups")
    rows_out = w_query.shape[0] // tp_count
    bf16, f32 = jnp.bfloat16, jnp.float32

    key_value = jnp.stack([key_head_rows, value_head_rows])
    window = {1: shifted(key_value, "seq", 1)}
    if reach > 1:
        window[reach] = shifted(key_value, "seq", reach)
    for d in range(2, reach):
        window[d] = shifted(window[d - 1], "seq", 1)
    far = tuple(range(reach, 1, -1))

    flags = attention_flags(doc_blocks, blocks, reach, place)

    def scratch(count, gradient):
        shapes = [
            pltpu.VMEM((blocks * lanes, HEAD_WIDTH), bf16),
            pltpu.VMEM((blocks * lanes, HEAD_WIDTH), bf16),
        ]
        if gradient:
            shapes.append(pltpu.VMEM((HEAD_WIDTH, count * rows), bf16))
        shapes += [pltpu.VMEM((2, count * rows, lanes), f32)] * 2
        if gradient:
            shapes += [pltpu.VMEM((count * rows, blocks * lanes), bf16)] * 2
        return shapes

    unit = 2 * rows * blocks * lanes * HEAD_WIDTH
    near_in = [query, output_gradient, key_head_rows, value_head_rows, window[1]]
    stats = [jax.ShapeDtypeStruct((blocks, lanes), f32)] * 3
    top, total, dot_total = kernel_call(
        functools.partial(near_stats_kernel, blocks, reach, heads),
        flags, near_in, stats, scratch(2, False), 4 * unit,
    )
    grads = {}
    kv_shape = (2, rows, HEAD_WIDTH)
    if far:
        stat, part, *far_grads = kernel_call(
            functools.partial(far_kernel, blocks, reach, heads, far),
            flags,
            [query, output_gradient, top, total, dot_total] + [window[d] for d in far],
            [
                jax.ShapeDtypeStruct((3, blocks, lanes), f32),
                jax.ShapeDtypeStruct((blocks, HEAD_WIDTH, lanes), f32),
            ]
            + [jax.ShapeDtypeStruct(kv_shape, bf16)] * len(far),
            scratch(len(far), True),
            5 * len(far) * unit,
        )
        grads = dict(zip(far, far_grads))
        near_extra = [stat, part]
    else:
        near_extra = [jnp.stack([top * SCALE_LOG2, 1.0 / total, dot_total / total])]
    own, grads[1], query_grad = kernel_call(
        functools.partial(near_kernel, blocks, reach, heads, bool(far)),
        flags,
        near_in + near_extra,
        [
            jax.ShapeDtypeStruct(kv_shape, f32),
            jax.ShapeDtypeStruct(kv_shape, f32),
            jax.ShapeDtypeStruct(query.shape, bf16),
        ],
        scratch(2, True),
        10 * unit,
    )

    if far:
        own = own + shifted(grads[reach], "seq", -reach).astype(f32)
        passed = None
        for d in range(reach - 1, 0, -1):
            sent = grads[d] if passed is None else (grads[d].astype(f32) + passed.astype(f32))
            passed = shifted(sent.astype(bf16), "seq", -1)
    else:
        passed = shifted(grads[1].astype(bf16), "seq", -1)
    key_value_grad = (own + passed.astype(f32)).astype(bf16)
    key_value_grad = jnp.concatenate([key_value_grad[0], key_value_grad[1]], axis=1)

    kv_weight = jnp.concatenate([key_weight, value_weight], axis=1)
    own_rows = lambda w: lax.dynamic_slice_in_dim(w, tp_place * rows_out, rows_out, axis=0)
    w_q = {0: own_rows(w_query)}
    w_kv = {0: own_rows(kv_weight)}
    for bits in range(1, tp_count):
        if bits == 1:
            w_q[bits] = swapped(weight_pieces(w_query, rows_out, tp_place, 0, 1, bits), "tp", bits)
            w_kv[bits] = swapped(weight_pieces(kv_weight, rows_out, tp_place, 0, 1, bits), "tp", bits)
        else:
            piece = weight_pieces(w_query, rows_out, tp_place, group_place, group_count, bits)
            w_q[bits] = gathered_rows(swapped(piece, "tp", bits), group_count, group_place)
            piece = weight_pieces(kv_weight, rows_out, tp_place, group_place, group_count, bits)
            w_kv[bits] = gathered_rows(swapped(piece, "tp", bits), group_count, group_place)

    def gathered(block):
        pieces = {0: block, 1: swapped(block, "tp", 1)}
        for bits in range(2, tp_count, 2):
            pieces[bits] = swapped(block, "tp", bits)
            pieces[bits + 1] = swapped(pieces[bits], "tp", 1)
        return pieces

    q_pieces = gathered(query_grad)
    kv_pieces = gathered(key_value_grad)
    result = None
    for pieces, weights in ((q_pieces, w_q), (kv_pieces, w_kv)):
        for bits in range(tp_count):
            part = lax.dot_general(pieces[bits], weights[bits], NT, preferred_element_type=f32)
            result = part if result is None else result + part
    return result.astype(bf16)


def solution(mesh):
    in_specs = (
        P(("groups", "seq"), "tp"),
        P(("groups", "seq"), "tp"),
        P(("groups", "seq"), "tp"),
        P(("groups", "seq"), "tp"),
        P(("groups", "seq"), None),
        P(None, "tp"),
        P(None, "tp"),
        P(None, "tp"),
    )
    out_specs = P(("groups", "seq"), "tp")
    return jax.shard_map(body, mesh=mesh, in_specs=in_specs, out_specs=out_specs, check_vma=False)
```

```python
import functools
import math

import jax
import jax.numpy as jnp
from jax import lax
from jax.experimental import pallas as pl
from jax.experimental.pallas import tpu as pltpu
from jax.sharding import PartitionSpec as P

HEAD_WIDTH = 128
BLOCK = 128
SCALE = HEAD_WIDTH ** (-0.5)
SCALE_LOG2 = SCALE * 1.4426950408889634
LOWEST = -1e30
NT = (((1,), (1,)), ((), ()))


def shifted(block, axis, distance):
    devices = range(lax.axis_size(axis))
    route = [(i - distance, i) for i in devices if i - distance in devices]
    return lax.ppermute(block, axis, route)


def swapped(block, axis, bits):
    return lax.ppermute(block, axis, [(i, i ^ bits) for i in range(lax.axis_size(axis))])


def key_range(distance, i, blocks, reach):
    if distance == 0:
        return 0, i + 1
    if distance == reach:
        return i, blocks
    return 0, blocks


def lane_range(distance, j, blocks, reach):
    if distance == 0:
        return j, blocks
    if distance == reach:
        return 0, j + 1
    return 0, blocks


def stack_heads(rows_ref, stack_ref, blocks, heads):
    for i in range(blocks):
        for h in range(heads):
            at = (i * heads + h) * BLOCK
            stack_ref[at : at + BLOCK, :] = rows_ref[
                i * BLOCK : (i + 1) * BLOCK, h * HEAD_WIDTH : (h + 1) * HEAD_WIDTH
            ]


def band_keep(offset, lanes):
    key_at = lax.broadcasted_iota(jnp.int32, (BLOCK, lanes), 0)
    query_at = lax.broadcasted_iota(jnp.int32, (BLOCK, lanes), 1) % BLOCK
    return key_at <= query_at if offset == 0 else key_at > query_at


def fold(tile, op):
    rows = tile.shape[0]
    total = tile[0:8]
    for at in range(8, rows, 8):
        total = op(total, tile[at : at + 8])
    return total


def keys_of(ref):
    return ref.at[:, 0:HEAD_WIDTH]


def values_of(ref):
    return ref.at[:, HEAD_WIDTH : 2 * HEAD_WIDTH]


def tiles_of(distances, i, blocks, reach):
    return [
        (c, d, j)
        for c, d in enumerate(distances)
        for j in range(*key_range(d, i, blocks, reach))
    ]


def score_pass(i, distances, blocks, reach, flag_ref, key_refs, value_refs, query_i, grad_i, s_ref, g_ref):
    rows = blocks * BLOCK
    top = None
    for c, d in enumerate(distances):
        low, high = key_range(d, i, blocks, reach)
        span = slice(low * BLOCK, high * BLOCK)
        at = slice(c * rows + low * BLOCK, c * rows + high * BLOCK)
        s_ref[at, :] = lax.dot_general(key_refs[c][span, :], query_i, NT, preferred_element_type=jnp.float32)
        g_ref[at, :] = lax.dot_general(value_refs[c][span, :], grad_i, NT, preferred_element_type=jnp.float32)
    for c, d, j in tiles_of(distances, i, blocks, reach):
        at = slice(c * rows + j * BLOCK, c * rows + (j + 1) * BLOCK)
        offset = d * blocks + i - j
        tile = s_ref[at, :]
        if offset < 2:
            tile = jnp.where(band_keep(offset, tile.shape[1]), tile, LOWEST)
            s_ref[at, :] = tile
        part = fold(tile, jnp.maximum)
        if offset > 0:
            part = jnp.where(flag_ref[i, d * blocks + j] != 0, part, LOWEST)
        top = part if top is None else jnp.maximum(top, part)
    return jnp.max(top, axis=0, keepdims=True)


def shift_of(flag_ref, i, d, j, blocks, base):
    if d * blocks + i - j == 0:
        return base
    return jnp.where(flag_ref[i, d * blocks + j] != 0, base, -LOWEST)


def weight_pass(i, distances, blocks, reach, flag_ref, s_ref, g_ref, base, keep):
    rows = blocks * BLOCK
    total = dot_total = None
    for c, d, j in tiles_of(distances, i, blocks, reach):
        at = slice(c * rows + j * BLOCK, c * rows + (j + 1) * BLOCK)
        weights = jnp.exp2(s_ref[at, :] * SCALE_LOG2 - shift_of(flag_ref, i, d, j, blocks, base))
        if keep:
            s_ref[at, :] = weights
        part = fold(weights, jnp.add)
        dot_part = fold(weights * g_ref[at, :], jnp.add)
        total = part if total is None else total + part
        dot_total = dot_part if dot_total is None else dot_total + dot_part
    return jnp.sum(total, axis=0, keepdims=True), jnp.sum(dot_total, axis=0, keepdims=True)


def key_value_sums(c, d, blocks, reach, lanes, p_ref, ds_ref, query_stack, grad_stack, out_ref):
    rows = blocks * BLOCK
    for j in range(blocks):
        low, high = lane_range(d, j, blocks, reach)
        at = slice(c * rows + j * BLOCK, c * rows + (j + 1) * BLOCK)
        span = slice(low * lanes, high * lanes)
        out = slice(j * BLOCK, (j + 1) * BLOCK)
        key_sum = jnp.dot(ds_ref[at, span], query_stack[span, :], preferred_element_type=jnp.float32)
        out_ref[out, 0:HEAD_WIDTH] = (key_sum * SCALE).astype(out_ref.dtype)
        value_sum = jnp.dot(p_ref[at, span], grad_stack[span, :], preferred_element_type=jnp.float32)
        out_ref[out, HEAD_WIDTH:] = value_sum.astype(out_ref.dtype)


def query_sum(i, distances, blocks, reach, lanes, key_turned, ds_ref):
    rows = blocks * BLOCK
    total = None
    for c, d in enumerate(distances):
        low, high = key_range(d, i, blocks, reach)
        at = slice(c * rows + low * BLOCK, c * rows + high * BLOCK)
        part = jnp.dot(
            key_turned[:, at], ds_ref[at, i * lanes : (i + 1) * lanes], preferred_element_type=jnp.float32
        )
        total = part if total is None else total + part
    return total


def near_stats_kernel(blocks, reach, heads, flag_ref, query_ref, grad_ref, k0, v0, kv1, m_ref, l_ref, r_ref, qs, gs, s_ref, g_ref):
    lanes = heads * BLOCK
    stack_heads(query_ref, qs, blocks, heads)
    stack_heads(grad_ref, gs, blocks, heads)
    for i in range(blocks):
        span = slice(i * lanes, (i + 1) * lanes)
        s_i, g_i = s_ref.at[i % 2], g_ref.at[i % 2]
        top = score_pass(
            i, (0, 1), blocks, reach, flag_ref, (k0, keys_of(kv1)), (v0, values_of(kv1)), qs[span, :], gs[span, :], s_i, g_i
        )
        total, dot_total = weight_pass(
            i, (0, 1), blocks, reach, flag_ref, s_i, g_i, top * SCALE_LOG2, False
        )
        m_ref[i : i + 1, :] = top
        l_ref[i : i + 1, :] = total
        r_ref[i : i + 1, :] = dot_total


def gradients(i, distances, blocks, reach, lanes, s_i, g_i, p_ref, ds_ref, inverse, delta):
    rows = blocks * BLOCK
    span = slice(i * lanes, (i + 1) * lanes)
    for c, d, j in tiles_of(distances, i, blocks, reach):
        at = slice(c * rows + j * BLOCK, c * rows + (j + 1) * BLOCK)
        probability = s_i[at, :] * inverse
        p_ref[at, span] = probability.astype(jnp.bfloat16)
        ds_ref[at, span] = (probability * (g_i[at, :] - delta)).astype(jnp.bfloat16)


def far_kernel(blocks, reach, heads, distances, middle, *refs):
    count = len(distances)
    flag_ref, query_ref, grad_ref, m_ref, l_ref, r_ref = refs[:6]
    kv_refs = refs[6 : 6 + count]
    stat_ref, part_ref = refs[6 + count : 8 + count]
    out_refs = refs[8 + count : 8 + count + len(middle)]
    qs, gs, kt, s_ref, g_ref, p_ref, ds_ref = refs[8 + count + len(middle) :]
    lanes = heads * BLOCK
    rows = blocks * BLOCK
    stack_heads(query_ref, qs, blocks, heads)
    stack_heads(grad_ref, gs, blocks, heads)
    keys = [keys_of(r) for r in kv_refs]
    values = [values_of(r) for r in kv_refs]
    for c in range(len(middle)):
        kt[:, c * rows : (c + 1) * rows] = keys[c][...].T
    for i in range(blocks):
        span = slice(i * lanes, (i + 1) * lanes)
        s_i, g_i = s_ref.at[i % 2], g_ref.at[i % 2]
        top = score_pass(
            i, distances, blocks, reach, flag_ref, keys, values, qs[span, :], gs[span, :], s_i, g_i
        )
        before = m_ref[i : i + 1, :]
        top = jnp.maximum(top, before)
        base = top * SCALE_LOG2
        total, dot_total = weight_pass(i, distances, blocks, reach, flag_ref, s_i, g_i, base, True)
        fade = jnp.exp2(before * SCALE_LOG2 - base)
        total = total + l_ref[i : i + 1, :] * fade
        dot_total = dot_total + r_ref[i : i + 1, :] * fade
        inverse = 1.0 / total
        delta = dot_total * inverse
        stat_ref[0, i : i + 1, :] = base
        stat_ref[1, i : i + 1, :] = inverse
        stat_ref[2, i : i + 1, :] = delta
        gradients(i, middle, blocks, reach, lanes, s_i, g_i, p_ref, ds_ref, inverse, delta)
    for c, d in enumerate(middle):
        key_value_sums(c, d, blocks, reach, lanes, p_ref, ds_ref, qs, gs, out_refs[c])
    for i in range(blocks):
        if middle:
            part_ref[i] = query_sum(i, middle, blocks, reach, lanes, kt, ds_ref)
        else:
            part_ref[i] = jnp.zeros_like(part_ref[i])


def gradient_kernel(blocks, reach, heads, distances, final, flag_ref, query_ref, grad_ref, stat_ref, part_ref, *refs):
    count = len(distances)
    keys, values = [], []
    for d in distances:
        if d == 0:
            keys.append(refs[0])
            values.append(refs[1])
            refs = refs[2:]
        else:
            keys.append(keys_of(refs[0]))
            values.append(values_of(refs[0]))
            refs = refs[1:]
    out_refs, query_out = refs[:count], refs[count]
    qs, gs, kt, s_ref, g_ref, p_ref, ds_ref = refs[count + 1 :]
    lanes = heads * BLOCK
    rows = blocks * BLOCK
    stack_heads(query_ref, qs, blocks, heads)
    stack_heads(grad_ref, gs, blocks, heads)
    for c in range(count):
        kt[:, c * rows : (c + 1) * rows] = keys[c][...].T
    for i in range(blocks):
        span = slice(i * lanes, (i + 1) * lanes)
        s_i, g_i = s_ref.at[i % 2], g_ref.at[i % 2]
        score_pass(i, distances, blocks, reach, flag_ref, keys, values, qs[span, :], gs[span, :], s_i, g_i)
        weight_pass(i, distances, blocks, reach, flag_ref, s_i, g_i, stat_ref[0, i : i + 1, :], True)
        gradients(
            i, distances, blocks, reach, lanes, s_i, g_i, p_ref, ds_ref,
            stat_ref[1, i : i + 1, :], stat_ref[2, i : i + 1, :],
        )
    for c, d in enumerate(distances):
        key_value_sums(c, d, blocks, reach, lanes, p_ref, ds_ref, qs, gs, out_refs[c])
    for i in range(blocks):
        total = part_ref[i] + query_sum(i, distances, blocks, reach, lanes, kt, ds_ref)
        if not final:
            query_out[i] = total
            continue
        total = total * SCALE
        for h in range(heads):
            query_out[i * BLOCK : (i + 1) * BLOCK, h * HEAD_WIDTH : (h + 1) * HEAD_WIDTH] = (
                total[:, h * BLOCK : (h + 1) * BLOCK].T.astype(query_out.dtype)
            )


def kernel_call(kernel, flags, arrays, outs, scratch, weight=0):
    size = sum(a.size * a.dtype.itemsize for a in arrays) + sum(a.size * a.dtype.itemsize for a in outs)
    held = sum(math.prod(s.shape) * jnp.dtype(s.dtype).itemsize for s in scratch)
    return pl.pallas_call(
        kernel,
        out_shape=outs,
        in_specs=[pl.BlockSpec(memory_space=pltpu.SMEM)] + [pl.BlockSpec(memory_space=pltpu.VMEM)] * len(arrays),
        out_specs=[pl.BlockSpec(memory_space=pltpu.VMEM)] * len(outs),
        scratch_shapes=scratch,
        compiler_params=pltpu.CompilerParams(vmem_limit_bytes=held + size + (8 << 20)),
        cost_estimate=pl.CostEstimate(flops=0, bytes_accessed=size * weight, transcendentals=0),
    )(flags, *arrays)


def attention_flags(doc_blocks, blocks, reach, place):
    query_ids = place * blocks + jnp.arange(blocks, dtype=jnp.int32)
    column = jnp.arange((reach + 1) * blocks, dtype=jnp.int32)
    key_ids = (place - column // blocks) * blocks + column % blocks
    behind = query_ids[:, None] - key_ids[None, :]
    listed = jnp.any(doc_blocks[:, :, None] == key_ids[None, None, :], axis=1)
    allowed = (key_ids[None, :] >= 0) & ((behind == 0) | (behind == 1) | ((behind >= 2) & listed))
    return allowed.astype(jnp.int32)


def pack_kernel(jobs, rows_ref, *refs):
    count = len(jobs)
    arrays, outs, sems = refs[: -count - 1], refs[-count - 1 : -1], refs[-1]
    copies = []
    for n, (members, size) in enumerate(jobs):
        start = pl.multiple_of(rows_ref[n], size)
        at = 0
        for member in members:
            array = arrays[member]
            width = array.shape[1]
            copies.append(
                pltpu.make_async_copy(
                    array.at[pl.ds(start, size), :], outs[n].at[:, at : at + width], sems.at[len(copies)]
                )
            )
            at += width
    for copy in copies:
        copy.start()
    for copy in copies:
        copy.wait()


def packed(jobs):
    arrays, plan = [], []
    for group, _, size in jobs:
        members = []
        for array in group:
            known = [n for n, a in enumerate(arrays) if a is array]
            if not known:
                arrays.append(array)
            members.append(known[0] if known else len(arrays) - 1)
        plan.append((tuple(members), size))
    starts = jnp.stack([jnp.asarray(start, jnp.int32) for _, start, _ in jobs])
    outs = [
        jax.ShapeDtypeStruct((size, sum(arrays[m].shape[1] for m in members)), arrays[0].dtype)
        for members, size in plan
    ]
    return pl.pallas_call(
        functools.partial(pack_kernel, plan),
        out_shape=outs,
        in_specs=[pl.BlockSpec(memory_space=pltpu.SMEM)] + [pl.BlockSpec(memory_space=pl.ANY)] * len(arrays),
        out_specs=[pl.BlockSpec(memory_space=pltpu.VMEM)] * len(outs),
        scratch_shapes=[pltpu.SemaphoreType.DMA((sum(len(members) for members, _ in plan),))],
        cost_estimate=pl.CostEstimate(
            flops=0, bytes_accessed=sum(2 * o.size * o.dtype.itemsize for o in outs), transcendentals=0
        ),
    )(starts, *arrays)


def first_product_kernel(tp_count, group_count, query_width, group_ref, *refs):
    acc_ref = refs[-1]
    product_kernel(tp_count, group_count, slice(0, query_width), group_ref, refs[:-1], None, acc_ref)


def last_product_kernel(tp_count, group_count, query_width, group_ref, acc_ref, *refs):
    product_kernel(tp_count, group_count, slice(query_width, None), group_ref, refs[:-1], acc_ref, refs[-1])


def product_kernel(tp_count, group_count, columns, group_ref, refs, acc_ref, out_ref):
    pieces, refs = refs[:tp_count], refs[tp_count:]
    whole, shares = refs[:2], refs[2:]
    share = whole[0].shape[0] // group_count
    group_place = group_ref[0]
    for step in range(group_count):
        source = lax.rem(group_place - step + group_count, group_count)
        span = pl.ds(pl.multiple_of(source * share, share), share)
        total = None if acc_ref is None else acc_ref[:, span]
        for bits in range(tp_count):
            if bits < 2:
                w = whole[bits][span, columns]
            else:
                w = shares[(bits - 2) * group_count + step][:, columns]
            part = lax.dot_general(pieces[bits][...], w, NT, preferred_element_type=jnp.float32)
            total = part if total is None else total + part
        out_ref[:, span] = total.astype(out_ref.dtype)


def body(query, key_head_rows, value_head_rows, output_gradient, doc_blocks, w_query, key_weight, value_weight):
    rows = query.shape[0]
    blocks = rows // BLOCK
    heads = query.shape[1] // key_head_rows.shape[1]
    lanes = heads * BLOCK
    reach = min(8, lax.axis_size("seq") - 1)
    place = lax.axis_index("seq")
    tp_count = lax.axis_size("tp")
    tp_place = lax.axis_index("tp")
    group_count = lax.axis_size("groups")
    group_place = lax.axis_index("groups")
    rows_out = w_query.shape[0] // tp_count
    share = rows_out // group_count
    bf16, f32 = jnp.bfloat16, jnp.float32

    weights = (w_query, key_weight, value_weight)
    own_kv = (key_head_rows, value_head_rows)

    def share_of(bits):
        return ((tp_place ^ bits) * rows_out + group_place * share, share)

    early = range(2, min(3, tp_count))
    late = range(3, tp_count)
    with jax.named_scope("pack_first"):
        key_value, *sent = packed([(own_kv, 0, rows)] + [(weights, *share_of(bits)) for bits in early])
    with jax.named_scope("kv_forward"):
        window = {1: shifted(key_value, "seq", 1)}
        if reach > 1:
            window[reach] = shifted(key_value, "seq", reach)
        for d in range(2, reach):
            window[d] = shifted(window[d - 1], "seq", 1)
        far = tuple(range(2, reach + 1))
    with jax.named_scope("pack_rest"):
        held, _ = lax.optimization_barrier((weights, key_value))
        pair_weights, own_weights, *more = packed(
            [(held, (tp_place ^ 1) * rows_out, rows_out), (held, tp_place * rows_out, rows_out)]
            + [(held, *share_of(bits)) for bits in late]
        )
    with jax.named_scope("weight_exchange"):
        whole = [own_weights, swapped(pair_weights, "tp", 1)]
        sent = [swapped(piece, "tp", bits) for bits, piece in zip([*early, *late], sent + more)]

    with jax.named_scope("flags"):
        flags = attention_flags(doc_blocks, blocks, reach, place)

    def scratch(count, gradient_count):
        stacks = [pltpu.VMEM((blocks * lanes, HEAD_WIDTH), bf16)] * 2
        tiles = [pltpu.VMEM((2, count * rows, lanes), f32)] * 2
        if not gradient_count:
            return stacks + tiles
        turned = [pltpu.VMEM((HEAD_WIDTH, gradient_count * rows), bf16)]
        return stacks + turned + tiles + [pltpu.VMEM((gradient_count * rows, blocks * lanes), bf16)] * 2

    near_in = [query, output_gradient, key_head_rows, value_head_rows, window[1]]
    stats = [jax.ShapeDtypeStruct((blocks, lanes), f32)] * 3
    near_in[0], pair_weights = lax.optimization_barrier((near_in[0], pair_weights))
    with jax.named_scope("near_stats"):
        top, total, dot_total = kernel_call(
            functools.partial(near_stats_kernel, blocks, reach, heads),
            flags, near_in, stats, scratch(2, 0),
        )
    grads = {}
    kv_shape = (rows, 2 * HEAD_WIDTH)
    part_shape = jax.ShapeDtypeStruct((blocks, HEAD_WIDTH, lanes), f32)
    if far:
        middle = far[:-1]
        with jax.named_scope("far_stats"):
            stat, part, *middle_grads = kernel_call(
                functools.partial(far_kernel, blocks, reach, heads, far, middle),
                flags,
                [query, output_gradient, top, total, dot_total] + [window[d] for d in far],
                [jax.ShapeDtypeStruct((3, blocks, lanes), f32), part_shape]
                + [jax.ShapeDtypeStruct(kv_shape, bf16)] * len(middle),
                scratch(len(far), max(len(middle), 1)),
            )
        grads = dict(zip(middle, middle_grads))
        with jax.named_scope("longest_gradients"):
            grads[reach], part = kernel_call(
                functools.partial(gradient_kernel, blocks, reach, heads, (reach,), False),
                flags,
                [query, output_gradient, stat, part, window[reach]],
                [jax.ShapeDtypeStruct(kv_shape, bf16), part_shape],
                scratch(1, 1),
            )
    else:
        stat = jnp.stack([top * SCALE_LOG2, 1.0 / total, dot_total / total])
        part = jnp.zeros(part_shape.shape, f32)
    def passed_on(piece, after):
        held, _ = lax.optimization_barrier((piece, after))
        moved = [piece]
        for step in range(1, group_count):
            route = [(i, (i + step) % group_count) for i in range(group_count)]
            moved.append(lax.ppermute(held, "groups", route))
        return moved

    with jax.named_scope("weight_exchange"):
        shares = passed_on(sent[0], stat) if sent else []

    with jax.named_scope("near_gradients"):
        own, grads[1], query_grad = kernel_call(
            functools.partial(gradient_kernel, blocks, reach, heads, (0, 1), True),
            flags,
            [query, output_gradient, stat, part, key_head_rows, value_head_rows, window[1]],
            [
                jax.ShapeDtypeStruct(kv_shape, f32),
                jax.ShapeDtypeStruct(kv_shape, f32),
                jax.ShapeDtypeStruct(query.shape, bf16),
            ],
            scratch(2, 2),
        )

    with jax.named_scope("weight_exchange"):
        for piece in sent[1:]:
            shares += passed_on(piece, query_grad)
    with jax.named_scope("kv_return"):
        if far:
            longest = shifted(grads[reach], "seq", -reach)
            passed = None
            for d in range(reach - 1, 0, -1):
                total = grads[d] if passed is None else (grads[d].astype(f32) + passed.astype(f32))
                total = total.astype(bf16)
                passed = shifted(total, "seq", -1)
        else:
            passed = shifted(grads[1].astype(bf16), "seq", -1)
        if far:
            longest, passed, *shares[1:2] = lax.optimization_barrier((longest, passed, *shares[1:2]))
            own = own + longest.astype(f32)
        key_value_grad = (own + passed.astype(f32)).astype(bf16)

    def gathered(block, before_last=None):
        pieces = {0: block, 1: swapped(block, "tp", 1)}
        for bits in range(2, tp_count, 2):
            pieces[bits] = swapped(block, "tp", bits)
            held = pieces[bits]
            if before_last is not None:
                held, _ = lax.optimization_barrier((held, before_last))
            pieces[bits + 1] = swapped(held, "tp", 1)
        return [pieces[bits] for bits in range(tp_count)]

    with jax.named_scope("query_grad_gather"):
        q_pieces = gathered(query_grad)
    group = jnp.full((1,), group_place, jnp.int32)
    out = jax.ShapeDtypeStruct((rows, rows_out), bf16)
    width = query.shape[1]
    with jax.named_scope("query_product"):
        (acc,) = kernel_call(
            functools.partial(first_product_kernel, tp_count, group_count, width),
            group, q_pieces + whole + shares, [jax.ShapeDtypeStruct((rows, rows_out), f32)], [], 1,
        )
    with jax.named_scope("kv_grad_gather"):
        kv_pieces = gathered(key_value_grad, acc)
    with jax.named_scope("kv_product"):
        (result,) = kernel_call(
            functools.partial(last_product_kernel, tp_count, group_count, width),
            group, [acc] + kv_pieces + whole + shares, [out], [], 1,
        )
    return result


def solution(mesh):
    in_specs = (
        P(("groups", "seq"), "tp"),
        P(("groups", "seq"), "tp"),
        P(("groups", "seq"), "tp"),
        P(("groups", "seq"), "tp"),
        P(("groups", "seq"), None),
        P(None, "tp"),
        P(None, "tp"),
        P(None, "tp"),
    )
    out_specs = P(("groups", "seq"), "tp")
    return jax.shard_map(body, mesh=mesh, in_specs=in_specs, out_specs=out_specs, check_vma=False)
```

```python
import functools
import math

import jax
import jax.numpy as jnp
from jax import lax
from jax.experimental import pallas as pl
from jax.experimental.pallas import tpu as pltpu
from jax.sharding import PartitionSpec as P

HEAD_WIDTH = 128
BLOCK = 128
SCALE = HEAD_WIDTH ** (-0.5)
SCALE_LOG2 = SCALE * 1.4426950408889634
LOWEST = -1e30
NT = (((1,), (1,)), ((), ()))


def shifted(block, axis, distance):
    devices = range(lax.axis_size(axis))
    route = [(i - distance, i) for i in devices if i - distance in devices]
    return lax.ppermute(block, axis, route)


def swapped(block, axis, bits):
    return lax.ppermute(block, axis, [(i, i ^ bits) for i in range(lax.axis_size(axis))])


def key_range(distance, i, blocks, reach):
    if distance == 0:
        return 0, i + 1
    if distance == reach:
        return i, blocks
    return 0, blocks


def lane_range(distance, j, blocks, reach):
    if distance == 0:
        return j, blocks
    if distance == reach:
        return 0, j + 1
    return 0, blocks


def stack_heads(rows_ref, stack_ref, blocks, heads):
    for i in range(blocks):
        for h in range(heads):
            at = (i * heads + h) * BLOCK
            stack_ref[at : at + BLOCK, :] = rows_ref[
                i * BLOCK : (i + 1) * BLOCK, h * HEAD_WIDTH : (h + 1) * HEAD_WIDTH
            ]


def band_keep(offset, lanes):
    key_at = lax.broadcasted_iota(jnp.int32, (BLOCK, lanes), 0)
    query_at = lax.broadcasted_iota(jnp.int32, (BLOCK, lanes), 1) % BLOCK
    return key_at <= query_at if offset == 0 else key_at > query_at


def fold(tile, op):
    rows = tile.shape[0]
    total = tile[0:8]
    for at in range(8, rows, 8):
        total = op(total, tile[at : at + 8])
    return total


def keys_of(ref):
    return ref.at[:, 0:HEAD_WIDTH]


def values_of(ref):
    return ref.at[:, HEAD_WIDTH : 2 * HEAD_WIDTH]


def tiles_of(distances, i, blocks, reach):
    return [
        (c, d, j)
        for c, d in enumerate(distances)
        for j in range(*key_range(d, i, blocks, reach))
    ]


def score_pass(i, distances, blocks, reach, flag_ref, key_refs, value_refs, query_i, grad_i, s_ref, g_ref):
    rows = blocks * BLOCK
    top = None
    for c, d in enumerate(distances):
        low, high = key_range(d, i, blocks, reach)
        span = slice(low * BLOCK, high * BLOCK)
        at = slice(c * rows + low * BLOCK, c * rows + high * BLOCK)
        s_ref[at, :] = lax.dot_general(key_refs[c][span, :], query_i, NT, preferred_element_type=jnp.float32)
        g_ref[at, :] = lax.dot_general(value_refs[c][span, :], grad_i, NT, preferred_element_type=jnp.float32)
    for c, d, j in tiles_of(distances, i, blocks, reach):
        at = slice(c * rows + j * BLOCK, c * rows + (j + 1) * BLOCK)
        offset = d * blocks + i - j
        tile = s_ref[at, :]
        if offset < 2:
            tile = jnp.where(band_keep(offset, tile.shape[1]), tile, LOWEST)
            s_ref[at, :] = tile
        part = fold(tile, jnp.maximum)
        if offset > 0:
            part = jnp.where(flag_ref[i, d * blocks + j] != 0, part, LOWEST)
        top = part if top is None else jnp.maximum(top, part)
    return jnp.max(top, axis=0, keepdims=True)


def shift_of(flag_ref, i, d, j, blocks, base):
    if d * blocks + i - j == 0:
        return base
    return jnp.where(flag_ref[i, d * blocks + j] != 0, base, -LOWEST)


def weight_pass(i, distances, blocks, reach, flag_ref, s_ref, g_ref, base, keep):
    rows = blocks * BLOCK
    total = dot_total = None
    for c, d, j in tiles_of(distances, i, blocks, reach):
        at = slice(c * rows + j * BLOCK, c * rows + (j + 1) * BLOCK)
        weights = jnp.exp2(s_ref[at, :] * SCALE_LOG2 - shift_of(flag_ref, i, d, j, blocks, base))
        if keep:
            s_ref[at, :] = weights
        part = fold(weights, jnp.add)
        dot_part = fold(weights * g_ref[at, :], jnp.add)
        total = part if total is None else total + part
        dot_total = dot_part if dot_total is None else dot_total + dot_part
    return jnp.sum(total, axis=0, keepdims=True), jnp.sum(dot_total, axis=0, keepdims=True)


def key_value_sums(c, d, blocks, reach, lanes, p_ref, ds_ref, query_stack, grad_stack, out_ref):
    rows = blocks * BLOCK
    for j in range(blocks):
        low, high = lane_range(d, j, blocks, reach)
        at = slice(c * rows + j * BLOCK, c * rows + (j + 1) * BLOCK)
        span = slice(low * lanes, high * lanes)
        out = slice(j * BLOCK, (j + 1) * BLOCK)
        key_sum = jnp.dot(ds_ref[at, span], query_stack[span, :], preferred_element_type=jnp.float32)
        out_ref[out, 0:HEAD_WIDTH] = (key_sum * SCALE).astype(out_ref.dtype)
        value_sum = jnp.dot(p_ref[at, span], grad_stack[span, :], preferred_element_type=jnp.float32)
        out_ref[out, HEAD_WIDTH:] = value_sum.astype(out_ref.dtype)


def query_sum(i, distances, blocks, reach, lanes, key_turned, ds_ref):
    rows = blocks * BLOCK
    total = None
    for c, d in enumerate(distances):
        low, high = key_range(d, i, blocks, reach)
        at = slice(c * rows + low * BLOCK, c * rows + high * BLOCK)
        part = jnp.dot(
            key_turned[:, at], ds_ref[at, i * lanes : (i + 1) * lanes], preferred_element_type=jnp.float32
        )
        total = part if total is None else total + part
    return total


def near_stats_kernel(blocks, reach, heads, flag_ref, query_ref, grad_ref, k0, v0, kv1, m_ref, l_ref, r_ref, qs, gs, s_ref, g_ref):
    lanes = heads * BLOCK
    stack_heads(query_ref, qs, blocks, heads)
    stack_heads(grad_ref, gs, blocks, heads)
    for i in range(blocks):
        span = slice(i * lanes, (i + 1) * lanes)
        s_i, g_i = s_ref.at[i % 2], g_ref.at[i % 2]
        top = score_pass(
            i, (0, 1), blocks, reach, flag_ref, (k0, keys_of(kv1)), (v0, values_of(kv1)), qs[span, :], gs[span, :], s_i, g_i
        )
        total, dot_total = weight_pass(
            i, (0, 1), blocks, reach, flag_ref, s_i, g_i, top * SCALE_LOG2, False
        )
        m_ref[i : i + 1, :] = top
        l_ref[i : i + 1, :] = total
        r_ref[i : i + 1, :] = dot_total


def gradients(i, distances, blocks, reach, lanes, s_i, g_i, p_ref, ds_ref, inverse, delta):
    rows = blocks * BLOCK
    span = slice(i * lanes, (i + 1) * lanes)
    for c, d, j in tiles_of(distances, i, blocks, reach):
        at = slice(c * rows + j * BLOCK, c * rows + (j + 1) * BLOCK)
        probability = s_i[at, :] * inverse
        p_ref[at, span] = probability.astype(jnp.bfloat16)
        ds_ref[at, span] = (probability * (g_i[at, :] - delta)).astype(jnp.bfloat16)


def far_kernel(blocks, reach, heads, distances, middle, *refs):
    count = len(distances)
    flag_ref, query_ref, grad_ref, m_ref, l_ref, r_ref = refs[:6]
    kv_refs = refs[6 : 6 + count]
    stat_ref, part_ref = refs[6 + count : 8 + count]
    out_refs = refs[8 + count : 8 + count + len(middle)]
    qs, gs, kt, s_ref, g_ref, p_ref, ds_ref = refs[8 + count + len(middle) :]
    lanes = heads * BLOCK
    rows = blocks * BLOCK
    stack_heads(query_ref, qs, blocks, heads)
    stack_heads(grad_ref, gs, blocks, heads)
    keys = [keys_of(r) for r in kv_refs]
    values = [values_of(r) for r in kv_refs]
    for c in range(len(middle)):
        kt[:, c * rows : (c + 1) * rows] = keys[c][...].T
    for i in range(blocks):
        span = slice(i * lanes, (i + 1) * lanes)
        s_i, g_i = s_ref.at[i % 2], g_ref.at[i % 2]
        top = score_pass(
            i, distances, blocks, reach, flag_ref, keys, values, qs[span, :], gs[span, :], s_i, g_i
        )
        before = m_ref[i : i + 1, :]
        top = jnp.maximum(top, before)
        base = top * SCALE_LOG2
        total, dot_total = weight_pass(i, distances, blocks, reach, flag_ref, s_i, g_i, base, True)
        fade = jnp.exp2(before * SCALE_LOG2 - base)
        total = total + l_ref[i : i + 1, :] * fade
        dot_total = dot_total + r_ref[i : i + 1, :] * fade
        inverse = 1.0 / total
        delta = dot_total * inverse
        stat_ref[0, i : i + 1, :] = base
        stat_ref[1, i : i + 1, :] = inverse
        stat_ref[2, i : i + 1, :] = delta
        gradients(i, middle, blocks, reach, lanes, s_i, g_i, p_ref, ds_ref, inverse, delta)
    for c, d in enumerate(middle):
        key_value_sums(c, d, blocks, reach, lanes, p_ref, ds_ref, qs, gs, out_refs[c])
    for i in range(blocks):
        if middle:
            part_ref[i] = query_sum(i, middle, blocks, reach, lanes, kt, ds_ref)
        else:
            part_ref[i] = jnp.zeros_like(part_ref[i])


def gradient_kernel(blocks, reach, heads, distances, final, flag_ref, query_ref, grad_ref, stat_ref, part_ref, *refs):
    count = len(distances)
    keys, values = [], []
    for d in distances:
        if d == 0:
            keys.append(refs[0])
            values.append(refs[1])
            refs = refs[2:]
        else:
            keys.append(keys_of(refs[0]))
            values.append(values_of(refs[0]))
            refs = refs[1:]
    out_refs, query_out = refs[:count], refs[count]
    qs, gs, kt, s_ref, g_ref, p_ref, ds_ref = refs[count + 1 :]
    lanes = heads * BLOCK
    rows = blocks * BLOCK
    stack_heads(query_ref, qs, blocks, heads)
    stack_heads(grad_ref, gs, blocks, heads)
    for c in range(count):
        kt[:, c * rows : (c + 1) * rows] = keys[c][...].T
    for i in range(blocks):
        span = slice(i * lanes, (i + 1) * lanes)
        s_i, g_i = s_ref.at[i % 2], g_ref.at[i % 2]
        score_pass(i, distances, blocks, reach, flag_ref, keys, values, qs[span, :], gs[span, :], s_i, g_i)
        weight_pass(i, distances, blocks, reach, flag_ref, s_i, g_i, stat_ref[0, i : i + 1, :], True)
        gradients(
            i, distances, blocks, reach, lanes, s_i, g_i, p_ref, ds_ref,
            stat_ref[1, i : i + 1, :], stat_ref[2, i : i + 1, :],
        )
    for c, d in enumerate(distances):
        key_value_sums(c, d, blocks, reach, lanes, p_ref, ds_ref, qs, gs, out_refs[c])
    for i in range(blocks):
        total = part_ref[i] + query_sum(i, distances, blocks, reach, lanes, kt, ds_ref)
        if not final:
            query_out[i] = total
            continue
        total = total * SCALE
        for h in range(heads):
            query_out[i * BLOCK : (i + 1) * BLOCK, h * HEAD_WIDTH : (h + 1) * HEAD_WIDTH] = (
                total[:, h * BLOCK : (h + 1) * BLOCK].T.astype(query_out.dtype)
            )


def kernel_call(kernel, flags, arrays, outs, scratch, weight=0, in_place=()):
    size = sum(a.size * a.dtype.itemsize for n, a in enumerate(arrays) if n not in in_place)
    size += sum(a.size * a.dtype.itemsize for a in outs)
    held = sum(math.prod(s.shape) * jnp.dtype(s.dtype).itemsize for s in scratch if hasattr(s, "dtype") and len(s.shape) > 1)
    return pl.pallas_call(
        kernel,
        out_shape=outs,
        in_specs=[pl.BlockSpec(memory_space=pltpu.SMEM)]
        + [pl.BlockSpec(memory_space=pl.ANY if n in in_place else pltpu.VMEM) for n in range(len(arrays))],
        out_specs=[pl.BlockSpec(memory_space=pltpu.VMEM)] * len(outs),
        scratch_shapes=scratch,
        compiler_params=pltpu.CompilerParams(vmem_limit_bytes=held + size + (8 << 20)),
        cost_estimate=pl.CostEstimate(flops=0, bytes_accessed=size * weight, transcendentals=0),
    )(flags, *arrays)


def attention_flags(doc_blocks, blocks, reach, place):
    query_ids = place * blocks + jnp.arange(blocks, dtype=jnp.int32)
    column = jnp.arange((reach + 1) * blocks, dtype=jnp.int32)
    key_ids = (place - column // blocks) * blocks + column % blocks
    behind = query_ids[:, None] - key_ids[None, :]
    listed = jnp.any(doc_blocks[:, :, None] == key_ids[None, None, :], axis=1)
    allowed = (key_ids[None, :] >= 0) & ((behind == 0) | (behind == 1) | ((behind >= 2) & listed))
    return allowed.astype(jnp.int32)


def pack_kernel(jobs, rows_ref, *refs):
    count = len(jobs)
    arrays, outs, sems = refs[: -count - 1], refs[-count - 1 : -1], refs[-1]
    copies = []
    for n, (members, size) in enumerate(jobs):
        start = pl.multiple_of(rows_ref[n], size)
        at = 0
        for member in members:
            array = arrays[member]
            width = array.shape[1]
            copies.append(
                pltpu.make_async_copy(
                    array.at[pl.ds(start, size), :], outs[n].at[:, at : at + width], sems.at[len(copies)]
                )
            )
            at += width
    for copy in copies:
        copy.start()
    for copy in copies:
        copy.wait()


def packed(jobs):
    arrays, plan = [], []
    for group, _, size in jobs:
        members = []
        for array in group:
            known = [n for n, a in enumerate(arrays) if a is array]
            if not known:
                arrays.append(array)
            members.append(known[0] if known else len(arrays) - 1)
        plan.append((tuple(members), size))
    starts = jnp.stack([jnp.asarray(start, jnp.int32) for _, start, _ in jobs])
    outs = [
        jax.ShapeDtypeStruct((size, sum(arrays[m].shape[1] for m in members)), arrays[0].dtype)
        for members, size in plan
    ]
    return pl.pallas_call(
        functools.partial(pack_kernel, plan),
        out_shape=outs,
        in_specs=[pl.BlockSpec(memory_space=pltpu.SMEM)] + [pl.BlockSpec(memory_space=pl.ANY)] * len(arrays),
        out_specs=[pl.BlockSpec(memory_space=pltpu.VMEM)] * len(outs),
        scratch_shapes=[pltpu.SemaphoreType.DMA((sum(len(members) for members, _ in plan),))],
        cost_estimate=pl.CostEstimate(
            flops=0, bytes_accessed=sum(2 * o.size * o.dtype.itemsize for o in outs), transcendentals=0
        ),
    )(starts, *arrays)


def product_kernel(tp_count, group_count, query_width, place_ref, *refs):
    q_pieces, kv_pieces, refs = refs[:tp_count], refs[tp_count : 2 * tp_count], refs[2 * tp_count :]
    out_ref, left, right, acc, sems = refs[-5:]
    whole, shares = refs[:2], refs[2:-5]
    rows_out = right.shape[1]
    share = rows_out // group_count
    copies = []
    for bits in range(tp_count):
        moves = [
            (q_pieces[bits], left.at[bits, :, 0:query_width]),
            (kv_pieces[bits], left.at[bits, :, query_width:]),
        ]
        if bits < 2:
            moves.append((whole[bits], right.at[bits]))
        else:
            for step in range(group_count):
                source = lax.rem(place_ref[0] - step + group_count, group_count)
                span = pl.ds(pl.multiple_of(source * share, share), share)
                moves.append((shares[(bits - 2) * group_count + step], right.at[bits, span, :]))
        copies.append(
            [pltpu.make_async_copy(a, b, sems.at[bits * (2 + group_count) + n]) for n, (a, b) in enumerate(moves)]
        )
    for group in copies:
        for copy in group:
            copy.start()
    for bits in range(tp_count):
        for copy in copies[bits]:
            copy.wait()
        for at in range(0, rows_out, rows_out // 4):
            span = slice(at, at + rows_out // 4)
            total = lax.dot_general(left[bits], right[bits, span, :], NT, preferred_element_type=jnp.float32)
            if bits:
                total = total + acc[:, span]
            if bits < tp_count - 1:
                acc[:, span] = total
            else:
                out_ref[:, span] = total.astype(out_ref.dtype)


def body(query, key_head_rows, value_head_rows, output_gradient, doc_blocks, w_query, key_weight, value_weight):
    rows = query.shape[0]
    blocks = rows // BLOCK
    heads = query.shape[1] // key_head_rows.shape[1]
    lanes = heads * BLOCK
    reach = min(8, lax.axis_size("seq") - 1)
    place = lax.axis_index("seq")
    tp_count = lax.axis_size("tp")
    tp_place = lax.axis_index("tp")
    group_count = lax.axis_size("groups")
    group_place = lax.axis_index("groups")
    rows_out = w_query.shape[0] // tp_count
    share = rows_out // group_count
    bf16, f32 = jnp.bfloat16, jnp.float32

    weights = (w_query, key_weight, value_weight)
    own_kv = (key_head_rows, value_head_rows)

    def share_of(bits):
        return ((tp_place ^ bits) * rows_out + group_place * share, share)

    early = range(2, min(3, tp_count))
    late = range(3, tp_count)
    with jax.named_scope("pack_first"):
        key_value, *sent = packed([(own_kv, 0, rows)] + [(weights, *share_of(bits)) for bits in early])
    with jax.named_scope("kv_forward"):
        window = {1: shifted(key_value, "seq", 1)}
        if reach > 1:
            window[reach] = shifted(key_value, "seq", reach)
        for d in range(2, reach):
            window[d] = shifted(window[d - 1], "seq", 1)
        far = tuple(range(2, reach + 1))
    with jax.named_scope("pack_rest"):
        held, _ = lax.optimization_barrier((weights, key_value))
        pair_weights, own_weights, *more = packed(
            [(held, (tp_place ^ 1) * rows_out, rows_out), (held, tp_place * rows_out, rows_out)]
            + [(held, *share_of(bits)) for bits in late]
        )
    with jax.named_scope("weight_exchange"):
        whole = [own_weights, swapped(pair_weights, "tp", 1)]
        sent = [swapped(piece, "tp", bits) for bits, piece in zip([*early, *late], sent + more)]

    with jax.named_scope("flags"):
        flags = attention_flags(doc_blocks, blocks, reach, place)

    def scratch(count, gradient_count):
        stacks = [pltpu.VMEM((blocks * lanes, HEAD_WIDTH), bf16)] * 2
        tiles = [pltpu.VMEM((2, count * rows, lanes), f32)] * 2
        if not gradient_count:
            return stacks + tiles
        turned = [pltpu.VMEM((HEAD_WIDTH, gradient_count * rows), bf16)]
        return stacks + turned + tiles + [pltpu.VMEM((gradient_count * rows, blocks * lanes), bf16)] * 2

    near_in = [query, output_gradient, key_head_rows, value_head_rows, window[1]]
    stats = [jax.ShapeDtypeStruct((blocks, lanes), f32)] * 3
    near_in[0], pair_weights = lax.optimization_barrier((near_in[0], pair_weights))
    with jax.named_scope("near_stats"):
        top, total, dot_total = kernel_call(
            functools.partial(near_stats_kernel, blocks, reach, heads),
            flags, near_in, stats, scratch(2, 0),
        )
    grads = {}
    kv_shape = (rows, 2 * HEAD_WIDTH)
    part_shape = jax.ShapeDtypeStruct((blocks, HEAD_WIDTH, lanes), f32)
    if far:
        middle = far[:-1]
        with jax.named_scope("far_stats"):
            stat, part, *middle_grads = kernel_call(
                functools.partial(far_kernel, blocks, reach, heads, far, middle),
                flags,
                [query, output_gradient, top, total, dot_total] + [window[d] for d in far],
                [jax.ShapeDtypeStruct((3, blocks, lanes), f32), part_shape]
                + [jax.ShapeDtypeStruct(kv_shape, bf16)] * len(middle),
                scratch(len(far), max(len(middle), 1)),
            )
        grads = dict(zip(middle, middle_grads))
        with jax.named_scope("longest_gradients"):
            grads[reach], part = kernel_call(
                functools.partial(gradient_kernel, blocks, reach, heads, (reach,), False),
                flags,
                [query, output_gradient, stat, part, window[reach]],
                [jax.ShapeDtypeStruct(kv_shape, bf16), part_shape],
                scratch(1, 1),
            )
    else:
        stat = jnp.stack([top * SCALE_LOG2, 1.0 / total, dot_total / total])
        part = jnp.zeros(part_shape.shape, f32)
    def passed_on(piece, after):
        held, _ = lax.optimization_barrier((piece, after))
        moved = [piece]
        for step in range(1, group_count):
            route = [(i, (i + step) % group_count) for i in range(group_count)]
            moved.append(lax.ppermute(held, "groups", route))
        return moved

    with jax.named_scope("weight_exchange"):
        shares = passed_on(sent[0], stat) if sent else []

    with jax.named_scope("near_gradients"):
        own, grads[1], query_grad = kernel_call(
            functools.partial(gradient_kernel, blocks, reach, heads, (0, 1), True),
            flags,
            [query, output_gradient, stat, part, key_head_rows, value_head_rows, window[1]],
            [
                jax.ShapeDtypeStruct(kv_shape, f32),
                jax.ShapeDtypeStruct(kv_shape, f32),
                jax.ShapeDtypeStruct(query.shape, bf16),
            ],
            scratch(2, 2),
        )

    with jax.named_scope("weight_exchange"):
        for piece in sent[1:]:
            shares += passed_on(piece, query_grad)
    with jax.named_scope("kv_return"):
        if far:
            longest = shifted(grads[reach], "seq", -reach)
            passed = None
            for d in range(reach - 1, 0, -1):
                total = grads[d] if passed is None else (grads[d].astype(f32) + passed.astype(f32))
                total = total.astype(bf16)
                passed = shifted(total, "seq", -1)
        else:
            passed = shifted(grads[1].astype(bf16), "seq", -1)
        if far:
            longest, passed, *shares[1:2] = lax.optimization_barrier((longest, passed, *shares[1:2]))
            own = own + longest.astype(f32)
        key_value_grad = (own + passed.astype(f32)).astype(bf16)

    def gathered(block, before_last=None):
        pieces = [block, swapped(block, "tp", 1)]
        for bits in range(2, tp_count, 2):
            pieces.append(swapped(block, "tp", bits))
            held = pieces[-1]
            if before_last is not None:
                held, _ = lax.optimization_barrier((held, before_last))
            pieces.append(swapped(held, "tp", 1))
        return pieces

    with jax.named_scope("query_grad_gather"):
        q_pieces = gathered(query_grad)
    with jax.named_scope("kv_grad_gather"):
        kv_pieces = gathered(key_value_grad, shares[-1])
    width = query.shape[1]
    total_width = width + 2 * HEAD_WIDTH
    arrays = q_pieces + kv_pieces + whole + shares
    with jax.named_scope("product"):
        (result,) = kernel_call(
            functools.partial(product_kernel, tp_count, group_count, width),
            jnp.full((1,), group_place, jnp.int32),
            arrays,
            [jax.ShapeDtypeStruct((rows, rows_out), bf16)],
            [
                pltpu.VMEM((tp_count, rows, total_width), bf16),
                pltpu.VMEM((tp_count, rows_out, total_width), bf16),
                pltpu.VMEM((rows, rows_out), f32),
                pltpu.SemaphoreType.DMA((tp_count * (2 + group_count),)),
            ],
            1,
            range(len(arrays)),
        )
    return result


def solution(mesh):
    in_specs = (
        P(("groups", "seq"), "tp"),
        P(("groups", "seq"), "tp"),
        P(("groups", "seq"), "tp"),
        P(("groups", "seq"), "tp"),
        P(("groups", "seq"), None),
        P(None, "tp"),
        P(None, "tp"),
        P(None, "tp"),
    )
    out_specs = P(("groups", "seq"), "tp")
    return jax.shard_map(body, mesh=mesh, in_specs=in_specs, out_specs=out_specs, check_vma=False)
```

```python
import functools
import math

import jax
import jax.numpy as jnp
from jax import lax
from jax.experimental import pallas as pl
from jax.experimental.pallas import tpu as pltpu
from jax.sharding import PartitionSpec as P

HEAD_WIDTH = 128
BLOCK = 128
SCALE = HEAD_WIDTH ** (-0.5)
SCALE_LOG2 = SCALE * 1.4426950408889634
LOWEST = -1e30
NT = (((1,), (1,)), ((), ()))


def shifted(block, axis, distance):
    devices = range(lax.axis_size(axis))
    route = [(i - distance, i) for i in devices if i - distance in devices]
    return lax.ppermute(block, axis, route)


def swapped(block, axis, bits):
    return lax.ppermute(block, axis, [(i, i ^ bits) for i in range(lax.axis_size(axis))])


def key_range(distance, i, blocks, reach):
    if distance == 0:
        return 0, i + 1
    if distance == reach:
        return i, blocks
    return 0, blocks


def lane_range(distance, j, blocks, reach):
    if distance == 0:
        return j, blocks
    if distance == reach:
        return 0, j + 1
    return 0, blocks


def stack_heads(rows_ref, stack_ref, blocks, heads):
    for i in range(blocks):
        for h in range(heads):
            at = (i * heads + h) * BLOCK
            stack_ref[at : at + BLOCK, :] = rows_ref[
                i * BLOCK : (i + 1) * BLOCK, h * HEAD_WIDTH : (h + 1) * HEAD_WIDTH
            ]


def band_keep(offset, lanes):
    key_at = lax.broadcasted_iota(jnp.int32, (BLOCK, lanes), 0)
    query_at = lax.broadcasted_iota(jnp.int32, (BLOCK, lanes), 1) % BLOCK
    return key_at <= query_at if offset == 0 else key_at > query_at


def fold(tile, op):
    rows = tile.shape[0]
    total = tile[0:8]
    for at in range(8, rows, 8):
        total = op(total, tile[at : at + 8])
    return total


def keys_of(ref):
    return ref.at[:, 0:HEAD_WIDTH]


def values_of(ref):
    return ref.at[:, HEAD_WIDTH : 2 * HEAD_WIDTH]


def tiles_of(distances, i, blocks, reach):
    return [
        (c, d, j)
        for c, d in enumerate(distances)
        for j in range(*key_range(d, i, blocks, reach))
    ]


def score_pass(i, distances, blocks, reach, flag_ref, key_refs, value_refs, query_i, grad_i, s_ref, g_ref):
    rows = blocks * BLOCK
    top = None
    for c, d in enumerate(distances):
        low, high = key_range(d, i, blocks, reach)
        span = slice(low * BLOCK, high * BLOCK)
        at = slice(c * rows + low * BLOCK, c * rows + high * BLOCK)
        s_ref[at, :] = lax.dot_general(key_refs[c][span, :], query_i, NT, preferred_element_type=jnp.float32)
        g_ref[at, :] = lax.dot_general(value_refs[c][span, :], grad_i, NT, preferred_element_type=jnp.float32)
    for c, d, j in tiles_of(distances, i, blocks, reach):
        at = slice(c * rows + j * BLOCK, c * rows + (j + 1) * BLOCK)
        offset = d * blocks + i - j
        tile = s_ref[at, :]
        if offset < 2:
            tile = jnp.where(band_keep(offset, tile.shape[1]), tile, LOWEST)
            s_ref[at, :] = tile
        part = fold(tile, jnp.maximum)
        if offset > 0:
            part = jnp.where(flag_ref[i, d * blocks + j] != 0, part, LOWEST)
        top = part if top is None else jnp.maximum(top, part)
    return jnp.max(top, axis=0, keepdims=True)


def shift_of(flag_ref, i, d, j, blocks, base):
    if d * blocks + i - j == 0:
        return base
    return jnp.where(flag_ref[i, d * blocks + j] != 0, base, -LOWEST)


def weight_pass(i, distances, blocks, reach, flag_ref, s_ref, g_ref, base, keep):
    rows = blocks * BLOCK
    total = dot_total = None
    for c, d, j in tiles_of(distances, i, blocks, reach):
        at = slice(c * rows + j * BLOCK, c * rows + (j + 1) * BLOCK)
        weights = jnp.exp2(s_ref[at, :] * SCALE_LOG2 - shift_of(flag_ref, i, d, j, blocks, base))
        if keep:
            s_ref[at, :] = weights
        part = fold(weights, jnp.add)
        dot_part = fold(weights * g_ref[at, :], jnp.add)
        total = part if total is None else total + part
        dot_total = dot_part if dot_total is None else dot_total + dot_part
    return jnp.sum(total, axis=0, keepdims=True), jnp.sum(dot_total, axis=0, keepdims=True)


def key_value_sums(c, d, blocks, reach, lanes, p_ref, ds_ref, query_stack, grad_stack, out_ref):
    rows = blocks * BLOCK
    ranges = [lane_range(d, j, blocks, reach) for j in range(blocks)]
    whole = all(r == (0, blocks) for r in ranges)
    for j, (low, high) in enumerate(ranges[:1] if whole else ranges):
        out = slice(j * BLOCK, rows if whole else (j + 1) * BLOCK)
        at = slice(c * rows + out.start, c * rows + out.stop)
        span = slice(low * lanes, high * lanes)
        key_sum = jnp.dot(ds_ref[at, span], query_stack[span, :], preferred_element_type=jnp.float32)
        out_ref[out, 0:HEAD_WIDTH] = (key_sum * SCALE).astype(out_ref.dtype)
        value_sum = jnp.dot(p_ref[at, span], grad_stack[span, :], preferred_element_type=jnp.float32)
        out_ref[out, HEAD_WIDTH:] = value_sum.astype(out_ref.dtype)


def query_sum(i, distances, blocks, reach, lanes, key_turned, ds_ref):
    rows = blocks * BLOCK
    total = None
    for c, d in enumerate(distances):
        low, high = key_range(d, i, blocks, reach)
        at = slice(c * rows + low * BLOCK, c * rows + high * BLOCK)
        part = jnp.dot(
            key_turned[:, at], ds_ref[at, i * lanes : (i + 1) * lanes], preferred_element_type=jnp.float32
        )
        total = part if total is None else total + part
    return total


def near_stats_kernel(blocks, reach, heads, flag_ref, query_ref, grad_ref, k0, v0, kv1, m_ref, l_ref, r_ref, qs, gs, s_ref, g_ref):
    lanes = heads * BLOCK
    stack_heads(query_ref, qs, blocks, heads)
    stack_heads(grad_ref, gs, blocks, heads)
    for i in range(blocks):
        span = slice(i * lanes, (i + 1) * lanes)
        s_i, g_i = s_ref.at[i % 2], g_ref.at[i % 2]
        top = score_pass(
            i, (0, 1), blocks, reach, flag_ref, (k0, keys_of(kv1)), (v0, values_of(kv1)), qs[span, :], gs[span, :], s_i, g_i
        )
        total, dot_total = weight_pass(
            i, (0, 1), blocks, reach, flag_ref, s_i, g_i, top * SCALE_LOG2, False
        )
        m_ref[i : i + 1, :] = top
        l_ref[i : i + 1, :] = total
        r_ref[i : i + 1, :] = dot_total


def gradients(i, distances, blocks, reach, lanes, s_i, g_i, p_ref, ds_ref, inverse, delta):
    rows = blocks * BLOCK
    span = slice(i * lanes, (i + 1) * lanes)
    for c, d, j in tiles_of(distances, i, blocks, reach):
        at = slice(c * rows + j * BLOCK, c * rows + (j + 1) * BLOCK)
        probability = s_i[at, :] * inverse
        p_ref[at, span] = probability.astype(jnp.bfloat16)
        ds_ref[at, span] = (probability * (g_i[at, :] - delta)).astype(jnp.bfloat16)


def far_kernel(blocks, reach, heads, distances, middle, *refs):
    count = len(distances)
    flag_ref, query_ref, grad_ref, m_ref, l_ref, r_ref = refs[:6]
    kv_refs = refs[6 : 6 + count]
    stat_ref, part_ref = refs[6 + count : 8 + count]
    out_refs = refs[8 + count : 8 + count + len(middle)]
    qs, gs, kt, s_ref, g_ref, p_ref, ds_ref = refs[8 + count + len(middle) :]
    lanes = heads * BLOCK
    rows = blocks * BLOCK
    stack_heads(query_ref, qs, blocks, heads)
    stack_heads(grad_ref, gs, blocks, heads)
    keys = [keys_of(r) for r in kv_refs]
    values = [values_of(r) for r in kv_refs]
    for c in range(len(middle)):
        kt[:, c * rows : (c + 1) * rows] = keys[c][...].T
    for i in range(blocks):
        span = slice(i * lanes, (i + 1) * lanes)
        s_i, g_i = s_ref.at[i % 2], g_ref.at[i % 2]
        top = score_pass(
            i, distances, blocks, reach, flag_ref, keys, values, qs[span, :], gs[span, :], s_i, g_i
        )
        before = m_ref[i : i + 1, :]
        top = jnp.maximum(top, before)
        base = top * SCALE_LOG2
        total, dot_total = weight_pass(i, distances, blocks, reach, flag_ref, s_i, g_i, base, True)
        fade = jnp.exp2(before * SCALE_LOG2 - base)
        total = total + l_ref[i : i + 1, :] * fade
        dot_total = dot_total + r_ref[i : i + 1, :] * fade
        inverse = 1.0 / total
        delta = dot_total * inverse
        stat_ref[0, i : i + 1, :] = base
        stat_ref[1, i : i + 1, :] = inverse
        stat_ref[2, i : i + 1, :] = delta
        gradients(i, middle, blocks, reach, lanes, s_i, g_i, p_ref, ds_ref, inverse, delta)
    for c, d in enumerate(middle):
        key_value_sums(c, d, blocks, reach, lanes, p_ref, ds_ref, qs, gs, out_refs[c])
    for i in range(blocks):
        if middle:
            part_ref[i] = query_sum(i, middle, blocks, reach, lanes, kt, ds_ref)
        else:
            part_ref[i] = jnp.zeros_like(part_ref[i])


def gradient_kernel(blocks, reach, heads, distances, final, flag_ref, query_ref, grad_ref, stat_ref, part_ref, *refs):
    count = len(distances)
    keys, values = [], []
    for d in distances:
        if d == 0:
            keys.append(refs[0])
            values.append(refs[1])
            refs = refs[2:]
        else:
            keys.append(keys_of(refs[0]))
            values.append(values_of(refs[0]))
            refs = refs[1:]
    out_refs, query_out = refs[:count], refs[count]
    qs, gs, kt, s_ref, g_ref, p_ref, ds_ref = refs[count + 1 :]
    lanes = heads * BLOCK
    rows = blocks * BLOCK
    stack_heads(query_ref, qs, blocks, heads)
    stack_heads(grad_ref, gs, blocks, heads)
    for c in range(count):
        kt[:, c * rows : (c + 1) * rows] = keys[c][...].T
    for i in range(blocks):
        span = slice(i * lanes, (i + 1) * lanes)
        s_i, g_i = s_ref.at[i % 2], g_ref.at[i % 2]
        score_pass(i, distances, blocks, reach, flag_ref, keys, values, qs[span, :], gs[span, :], s_i, g_i)
        weight_pass(i, distances, blocks, reach, flag_ref, s_i, g_i, stat_ref[0, i : i + 1, :], True)
        gradients(
            i, distances, blocks, reach, lanes, s_i, g_i, p_ref, ds_ref,
            stat_ref[1, i : i + 1, :], stat_ref[2, i : i + 1, :],
        )
    for c, d in enumerate(distances):
        key_value_sums(c, d, blocks, reach, lanes, p_ref, ds_ref, qs, gs, out_refs[c])
    for i in range(blocks):
        total = part_ref[i] + query_sum(i, distances, blocks, reach, lanes, kt, ds_ref)
        if not final:
            query_out[i] = total
            continue
        total = total * SCALE
        for h in range(heads):
            query_out[i * BLOCK : (i + 1) * BLOCK, h * HEAD_WIDTH : (h + 1) * HEAD_WIDTH] = (
                total[:, h * BLOCK : (h + 1) * BLOCK].T.astype(query_out.dtype)
            )


def kernel_call(kernel, flags, arrays, outs, scratch, weight=0, in_place=()):
    size = sum(a.size * a.dtype.itemsize for n, a in enumerate(arrays) if n not in in_place)
    size += sum(a.size * a.dtype.itemsize for a in outs)
    held = sum(math.prod(s.shape) * jnp.dtype(s.dtype).itemsize for s in scratch if hasattr(s, "dtype") and len(s.shape) > 1)
    return pl.pallas_call(
        kernel,
        out_shape=outs,
        in_specs=[pl.BlockSpec(memory_space=pltpu.SMEM)]
        + [pl.BlockSpec(memory_space=pl.ANY if n in in_place else pltpu.VMEM) for n in range(len(arrays))],
        out_specs=[pl.BlockSpec(memory_space=pltpu.VMEM)] * len(outs),
        scratch_shapes=scratch,
        compiler_params=pltpu.CompilerParams(vmem_limit_bytes=held + size + (8 << 20)),
        cost_estimate=pl.CostEstimate(flops=0, bytes_accessed=size * weight, transcendentals=0),
    )(flags, *arrays)


def attention_flags(doc_blocks, blocks, reach, place):
    query_ids = place * blocks + jnp.arange(blocks, dtype=jnp.int32)
    column = jnp.arange((reach + 1) * blocks, dtype=jnp.int32)
    key_ids = (place - column // blocks) * blocks + column % blocks
    behind = query_ids[:, None] - key_ids[None, :]
    listed = jnp.any(doc_blocks[:, :, None] == key_ids[None, None, :], axis=1)
    allowed = (key_ids[None, :] >= 0) & ((behind == 0) | (behind == 1) | ((behind >= 2) & listed))
    return allowed.astype(jnp.int32)


def pack_kernel(jobs, rows_ref, *refs):
    count = len(jobs)
    arrays, outs, sems = refs[: -count - 1], refs[-count - 1 : -1], refs[-1]
    copies = []
    for n, (members, size) in enumerate(jobs):
        start = pl.multiple_of(rows_ref[n], size)
        at = 0
        for member in members:
            array = arrays[member]
            width = array.shape[1]
            copies.append(
                pltpu.make_async_copy(
                    array.at[pl.ds(start, size), :], outs[n].at[:, at : at + width], sems.at[len(copies)]
                )
            )
            at += width
    for copy in copies:
        copy.start()
    for copy in copies:
        copy.wait()


def packed(jobs):
    arrays, plan = [], []
    for group, _, size in jobs:
        members = []
        for array in group:
            known = [n for n, a in enumerate(arrays) if a is array]
            if not known:
                arrays.append(array)
            members.append(known[0] if known else len(arrays) - 1)
        plan.append((tuple(members), size))
    starts = jnp.stack([jnp.asarray(start, jnp.int32) for _, start, _ in jobs])
    outs = [
        jax.ShapeDtypeStruct((size, sum(arrays[m].shape[1] for m in members)), arrays[0].dtype)
        for members, size in plan
    ]
    return pl.pallas_call(
        functools.partial(pack_kernel, plan),
        out_shape=outs,
        in_specs=[pl.BlockSpec(memory_space=pltpu.SMEM)] + [pl.BlockSpec(memory_space=pl.ANY)] * len(arrays),
        out_specs=[pl.BlockSpec(memory_space=pltpu.VMEM)] * len(outs),
        scratch_shapes=[pltpu.SemaphoreType.DMA((sum(len(members) for members, _ in plan),))],
        cost_estimate=pl.CostEstimate(
            flops=0, bytes_accessed=sum(2 * o.size * o.dtype.itemsize for o in outs), transcendentals=0
        ),
    )(starts, *arrays)


def product_kernel(peers, group_count, query_width, last, place_ref, *refs):
    before, refs = (refs[0], refs[1:]) if last else (None, refs)
    out_ref, left, right, acc, sems = refs[-5:]
    rows_out = right.shape[1]
    copies = []
    at = 0
    for n, (parts, low, high) in enumerate(peers):
        moves = []
        for piece, first in parts:
            width = refs[piece].shape[1]
            moves.append((refs[piece], left.at[n, :, first : first + width]))
        columns = slice(parts[0][1], parts[-1][1] + refs[parts[-1][0]].shape[1])
        weights = refs[low:high]
        share = rows_out // len(weights)
        for step, array in enumerate(weights):
            source = lax.rem(place_ref[0] - step + group_count, group_count) if len(weights) > 1 else 0
            span = pl.ds(pl.multiple_of(source * share, share), share)
            moves.append((array.at[:, columns], right.at[n, span, columns]))
        copies.append([pltpu.make_async_copy(a, b, sems.at[at + m]) for m, (a, b) in enumerate(moves)])
        at += len(moves)
    if last:
        copies[0].append(pltpu.make_async_copy(before, acc, sems.at[at]))
    for group in copies:
        for copy in group:
            copy.start()
    for n, (parts, _, _) in enumerate(peers):
        for copy in copies[n]:
            copy.wait()
        columns = slice(parts[0][1], parts[-1][1] + refs[parts[-1][0]].shape[1])
        for at in range(0, rows_out, rows_out // 4):
            span = slice(at, at + rows_out // 4)
            total = lax.dot_general(
                left[n, :, columns], right[n, span, columns], NT, preferred_element_type=jnp.float32
            )
            if n or last:
                total = total + acc[:, span]
            if n < len(peers) - 1:
                acc[:, span] = total
            else:
                out_ref[:, span] = total.astype(out_ref.dtype)


def body(query, key_head_rows, value_head_rows, output_gradient, doc_blocks, w_query, key_weight, value_weight):
    rows = query.shape[0]
    blocks = rows // BLOCK
    heads = query.shape[1] // key_head_rows.shape[1]
    lanes = heads * BLOCK
    reach = min(8, lax.axis_size("seq") - 1)
    place = lax.axis_index("seq")
    tp_count = lax.axis_size("tp")
    tp_place = lax.axis_index("tp")
    group_count = lax.axis_size("groups")
    group_place = lax.axis_index("groups")
    rows_out = w_query.shape[0] // tp_count
    share = rows_out // group_count
    bf16, f32 = jnp.bfloat16, jnp.float32

    weights = (w_query, key_weight, value_weight)
    own_kv = (key_head_rows, value_head_rows)

    def share_of(bits):
        return ((tp_place ^ bits) * rows_out + group_place * share, share)

    early = range(2, min(3, tp_count))
    late = range(3, tp_count)
    with jax.named_scope("pack_first"):
        key_value, *sent = packed([(own_kv, 0, rows)] + [(weights, *share_of(bits)) for bits in early])
    with jax.named_scope("kv_forward"):
        window = {1: shifted(key_value, "seq", 1)}
        if reach > 1:
            window[reach] = shifted(key_value, "seq", reach)
        for d in range(2, reach):
            window[d] = shifted(window[d - 1], "seq", 1)
        far = tuple(range(2, reach + 1))
    with jax.named_scope("pack_rest"):
        held, _ = lax.optimization_barrier((weights, key_value))
        pair_weights, own_weights, *more = packed(
            [(held, (tp_place ^ 1) * rows_out, rows_out), (held, tp_place * rows_out, rows_out)]
            + [(held, *share_of(bits)) for bits in late]
        )
    with jax.named_scope("weight_exchange"):
        whole = [own_weights, swapped(pair_weights, "tp", 1)]
        sent = [swapped(piece, "tp", bits) for bits, piece in zip([*early, *late], sent + more)]

    with jax.named_scope("flags"):
        flags = attention_flags(doc_blocks, blocks, reach, place)

    def scratch(count, gradient_count):
        stacks = [pltpu.VMEM((blocks * lanes, HEAD_WIDTH), bf16)] * 2
        tiles = [pltpu.VMEM((2, count * rows, lanes), f32)] * 2
        if not gradient_count:
            return stacks + tiles
        turned = [pltpu.VMEM((HEAD_WIDTH, gradient_count * rows), bf16)]
        return stacks + turned + tiles + [pltpu.VMEM((gradient_count * rows, blocks * lanes), bf16)] * 2

    near_in = [query, output_gradient, key_head_rows, value_head_rows, window[1]]
    stats = [jax.ShapeDtypeStruct((blocks, lanes), f32)] * 3
    near_in[0], pair_weights = lax.optimization_barrier((near_in[0], pair_weights))
    with jax.named_scope("near_stats"):
        top, total, dot_total = kernel_call(
            functools.partial(near_stats_kernel, blocks, reach, heads),
            flags, near_in, stats, scratch(2, 0),
        )
    grads = {}
    kv_shape = (rows, 2 * HEAD_WIDTH)
    part_shape = jax.ShapeDtypeStruct((blocks, HEAD_WIDTH, lanes), f32)
    if far:
        middle = far[:-1]
        with jax.named_scope("far_stats"):
            stat, part, *middle_grads = kernel_call(
                functools.partial(far_kernel, blocks, reach, heads, far, middle),
                flags,
                [query, output_gradient, top, total, dot_total] + [window[d] for d in far],
                [jax.ShapeDtypeStruct((3, blocks, lanes), f32), part_shape]
                + [jax.ShapeDtypeStruct(kv_shape, bf16)] * len(middle),
                scratch(len(far), max(len(middle), 1)),
            )
        grads = dict(zip(middle, middle_grads))
        with jax.named_scope("longest_gradients"):
            grads[reach], part = kernel_call(
                functools.partial(gradient_kernel, blocks, reach, heads, (reach,), False),
                flags,
                [query, output_gradient, stat, part, window[reach]],
                [jax.ShapeDtypeStruct(kv_shape, bf16), part_shape],
                scratch(1, 1),
            )
    else:
        stat = jnp.stack([top * SCALE_LOG2, 1.0 / total, dot_total / total])
        part = jnp.zeros(part_shape.shape, f32)
    def passed_on(piece, after):
        held, _ = lax.optimization_barrier((piece, after))
        moved = [piece]
        for step in range(1, group_count):
            route = [(i, (i + step) % group_count) for i in range(group_count)]
            moved.append(lax.ppermute(held, "groups", route))
        return moved

    with jax.named_scope("weight_exchange"):
        shares = passed_on(sent[0], stat) if sent else []

    with jax.named_scope("near_gradients"):
        own, grads[1], query_grad = kernel_call(
            functools.partial(gradient_kernel, blocks, reach, heads, (0, 1), True),
            flags,
            [query, output_gradient, stat, part, key_head_rows, value_head_rows, window[1]],
            [
                jax.ShapeDtypeStruct(kv_shape, f32),
                jax.ShapeDtypeStruct(kv_shape, f32),
                jax.ShapeDtypeStruct(query.shape, bf16),
            ],
            scratch(2, 2),
        )

    with jax.named_scope("weight_exchange"):
        for piece in sent[1:]:
            shares += passed_on(piece, query_grad)
    with jax.named_scope("kv_return"):
        if far:
            longest = shifted(grads[reach], "seq", -reach)
            passed = None
            for d in range(reach - 1, 0, -1):
                total = grads[d] if passed is None else (grads[d].astype(f32) + passed.astype(f32))
                total = total.astype(bf16)
                passed = shifted(total, "seq", -1)
        else:
            passed = shifted(grads[1].astype(bf16), "seq", -1)
        if far:
            longest, passed, *shares[1:2] = lax.optimization_barrier((longest, passed, *shares[1:2]))
            own = own + longest.astype(f32)
        key_value_grad = (own + passed.astype(f32)).astype(bf16)

    def gathered(block, before_last=None):
        pieces = [block, swapped(block, "tp", 1)]
        for bits in range(2, tp_count, 2):
            pieces.append(swapped(block, "tp", bits))
            held = pieces[-1]
            if before_last is not None:
                held, _ = lax.optimization_barrier((held, before_last))
            pieces.append(swapped(held, "tp", 1))
        return pieces

    with jax.named_scope("query_grad_gather"):
        q_pieces = gathered(query_grad)
    width = query.shape[1]
    total_width = width + 2 * HEAD_WIDTH
    place_ids = jnp.full((1,), group_place, jnp.int32)

    def product(scope, before, entries, out_type):
        arrays = [] if before is None else [before]
        peers = []
        for parts, weights in entries:
            placed = []
            for piece, first in parts:
                placed.append((len(arrays) - (before is not None), first))
                arrays.append(piece)
            low = len(arrays) - (before is not None)
            arrays += weights
            peers.append((tuple(placed), low, low + len(weights)))
        count = sum(len(parts) + len(weights) for parts, weights in entries) + 1
        with jax.named_scope(scope):
            (result,) = kernel_call(
                functools.partial(product_kernel, peers, group_count, width, before is not None),
                place_ids,
                arrays,
                [jax.ShapeDtypeStruct((rows, rows_out), out_type)],
                [
                    pltpu.VMEM((len(entries), rows, total_width), bf16),
                    pltpu.VMEM((len(entries), rows_out, total_width), bf16),
                    pltpu.VMEM((rows, rows_out), f32),
                    pltpu.SemaphoreType.DMA((count,)),
                ],
                0,
                range(len(arrays)),
            )
        return result

    sets = [[whole[0]], [whole[1]]]
    sets += [shares[at : at + group_count] for at in range(0, len(shares), group_count)]
    acc = product(
        "query_product", None, [([(q_pieces[bits], 0)], sets[bits]) for bits in range(tp_count - 1)], f32
    )
    with jax.named_scope("kv_grad_gather"):
        kv_pieces = gathered(key_value_grad, [acc] + shares[-1:])
    entries = [([(kv_pieces[bits], width)], sets[bits]) for bits in range(tp_count - 1)]
    entries.append(([(q_pieces[-1], 0), (kv_pieces[-1], width)], sets[-1]))
    return product("last_product", acc, entries, bf16)


def solution(mesh):
    in_specs = (
        P(("groups", "seq"), "tp"),
        P(("groups", "seq"), "tp"),
        P(("groups", "seq"), "tp"),
        P(("groups", "seq"), "tp"),
        P(("groups", "seq"), None),
        P(None, "tp"),
        P(None, "tp"),
        P(None, "tp"),
    )
    out_specs = P(("groups", "seq"), "tp")
    return jax.shard_map(body, mesh=mesh, in_specs=in_specs, out_specs=out_specs, check_vma=False)
```

```python
import functools
import math

import jax
import jax.numpy as jnp
from jax import lax
from jax.experimental import pallas as pl
from jax.experimental.pallas import tpu as pltpu
from jax.sharding import PartitionSpec as P

HEAD_WIDTH = 128
BLOCK = 128
SCALE = HEAD_WIDTH ** (-0.5)
SCALE_LOG2 = SCALE * 1.4426950408889634
LOWEST = -1e30
NT = (((1,), (1,)), ((), ()))


def shifted(block, axis, distance):
    devices = range(lax.axis_size(axis))
    route = [(i - distance, i) for i in devices if i - distance in devices]
    return lax.ppermute(block, axis, route)


def swapped(block, axis, bits):
    return lax.ppermute(block, axis, [(i, i ^ bits) for i in range(lax.axis_size(axis))])


def key_range(distance, i, blocks, reach):
    if distance == 0:
        return 0, i + 1
    if distance == reach:
        return i, blocks
    return 0, blocks


def lane_range(distance, j, blocks, reach):
    if distance == 0:
        return j, blocks
    if distance == reach:
        return 0, j + 1
    return 0, blocks


def stack_heads(rows_ref, stack_ref, blocks, heads):
    for i in range(blocks):
        for h in range(heads):
            at = (i * heads + h) * BLOCK
            stack_ref[at : at + BLOCK, :] = rows_ref[
                i * BLOCK : (i + 1) * BLOCK, h * HEAD_WIDTH : (h + 1) * HEAD_WIDTH
            ]


def band_keep(offset, lanes):
    key_at = lax.broadcasted_iota(jnp.int32, (BLOCK, lanes), 0)
    query_at = lax.broadcasted_iota(jnp.int32, (BLOCK, lanes), 1) % BLOCK
    return key_at <= query_at if offset == 0 else key_at > query_at


def fold(tile, op):
    rows = tile.shape[0]
    total = tile[0:8]
    for at in range(8, rows, 8):
        total = op(total, tile[at : at + 8])
    return total


def keys_of(ref):
    return ref.at[:, 0:HEAD_WIDTH]


def values_of(ref):
    return ref.at[:, HEAD_WIDTH : 2 * HEAD_WIDTH]


def tiles_of(distances, i, blocks, reach):
    return [
        (c, d, j)
        for c, d in enumerate(distances)
        for j in range(*key_range(d, i, blocks, reach))
    ]


def score_pass(i, distances, blocks, reach, flag_ref, key_refs, value_refs, query_i, grad_i, s_ref, g_ref):
    rows = blocks * BLOCK
    top = None
    for c, d in enumerate(distances):
        low, high = key_range(d, i, blocks, reach)
        span = slice(low * BLOCK, high * BLOCK)
        at = slice(c * rows + low * BLOCK, c * rows + high * BLOCK)
        s_ref[at, :] = lax.dot_general(key_refs[c][span, :], query_i, NT, preferred_element_type=jnp.float32)
        g_ref[at, :] = lax.dot_general(value_refs[c][span, :], grad_i, NT, preferred_element_type=jnp.float32)
    for c, d, j in tiles_of(distances, i, blocks, reach):
        at = slice(c * rows + j * BLOCK, c * rows + (j + 1) * BLOCK)
        offset = d * blocks + i - j
        tile = s_ref[at, :]
        if offset < 2:
            tile = jnp.where(band_keep(offset, tile.shape[1]), tile, LOWEST)
            s_ref[at, :] = tile
        part = fold(tile, jnp.maximum)
        if offset > 0:
            part = jnp.where(flag_ref[i, d * blocks + j] != 0, part, LOWEST)
        top = part if top is None else jnp.maximum(top, part)
    return jnp.max(top, axis=0, keepdims=True)


def shift_of(flag_ref, i, d, j, blocks, base):
    if d * blocks + i - j == 0:
        return base
    return jnp.where(flag_ref[i, d * blocks + j] != 0, base, -LOWEST)


def weight_pass(i, distances, blocks, reach, flag_ref, s_ref, g_ref, base, keep):
    rows = blocks * BLOCK
    total = dot_total = None
    for c, d, j in tiles_of(distances, i, blocks, reach):
        at = slice(c * rows + j * BLOCK, c * rows + (j + 1) * BLOCK)
        weights = jnp.exp2(s_ref[at, :] * SCALE_LOG2 - shift_of(flag_ref, i, d, j, blocks, base))
        if keep:
            s_ref[at, :] = weights
        part = fold(weights, jnp.add)
        dot_part = fold(weights * g_ref[at, :], jnp.add)
        total = part if total is None else total + part
        dot_total = dot_part if dot_total is None else dot_total + dot_part
    return jnp.sum(total, axis=0, keepdims=True), jnp.sum(dot_total, axis=0, keepdims=True)


def key_value_sums(c, d, blocks, reach, lanes, p_ref, ds_ref, query_stack, grad_stack, out_ref):
    rows = blocks * BLOCK
    ranges = [lane_range(d, j, blocks, reach) for j in range(blocks)]
    whole = all(r == (0, blocks) for r in ranges)
    for j, (low, high) in enumerate(ranges[:1] if whole else ranges):
        out = slice(j * BLOCK, rows if whole else (j + 1) * BLOCK)
        at = slice(c * rows + out.start, c * rows + out.stop)
        span = slice(low * lanes, high * lanes)
        key_sum = jnp.dot(ds_ref[at, span], query_stack[span, :], preferred_element_type=jnp.float32)
        out_ref[out, 0:HEAD_WIDTH] = (key_sum * SCALE).astype(out_ref.dtype)
        value_sum = jnp.dot(p_ref[at, span], grad_stack[span, :], preferred_element_type=jnp.float32)
        out_ref[out, HEAD_WIDTH:] = value_sum.astype(out_ref.dtype)


def query_sum(i, distances, blocks, reach, lanes, key_turned, ds_ref):
    rows = blocks * BLOCK
    total = None
    for c, d in enumerate(distances):
        low, high = key_range(d, i, blocks, reach)
        at = slice(c * rows + low * BLOCK, c * rows + high * BLOCK)
        part = jnp.dot(
            key_turned[:, at], ds_ref[at, i * lanes : (i + 1) * lanes], preferred_element_type=jnp.float32
        )
        total = part if total is None else total + part
    return total


def near_stats_kernel(blocks, reach, heads, flag_ref, query_ref, grad_ref, k0, v0, kv1, m_ref, l_ref, r_ref, qs, gs, s_ref, g_ref):
    lanes = heads * BLOCK
    stack_heads(query_ref, qs, blocks, heads)
    stack_heads(grad_ref, gs, blocks, heads)
    for i in range(blocks):
        span = slice(i * lanes, (i + 1) * lanes)
        s_i, g_i = s_ref.at[i % 2], g_ref.at[i % 2]
        top = score_pass(
            i, (0, 1), blocks, reach, flag_ref, (k0, keys_of(kv1)), (v0, values_of(kv1)), qs[span, :], gs[span, :], s_i, g_i
        )
        total, dot_total = weight_pass(
            i, (0, 1), blocks, reach, flag_ref, s_i, g_i, top * SCALE_LOG2, False
        )
        m_ref[i : i + 1, :] = top
        l_ref[i : i + 1, :] = total
        r_ref[i : i + 1, :] = dot_total


def gradients(i, distances, blocks, reach, lanes, s_i, g_i, p_ref, ds_ref, inverse, delta):
    rows = blocks * BLOCK
    span = slice(i * lanes, (i + 1) * lanes)
    for c, d, j in tiles_of(distances, i, blocks, reach):
        at = slice(c * rows + j * BLOCK, c * rows + (j + 1) * BLOCK)
        probability = s_i[at, :] * inverse
        p_ref[at, span] = probability.astype(jnp.bfloat16)
        ds_ref[at, span] = (probability * (g_i[at, :] - delta)).astype(jnp.bfloat16)


def far_kernel(blocks, reach, heads, distances, middle, *refs):
    count = len(distances)
    flag_ref, qs, gs, m_ref, l_ref, r_ref = refs[:6]
    kv_refs = refs[6 : 6 + count]
    stat_ref, part_ref = refs[6 + count : 8 + count]
    out_refs = refs[8 + count : 8 + count + len(middle)]
    kt, s_ref, g_ref, p_ref, ds_ref = refs[8 + count + len(middle) :]
    lanes = heads * BLOCK
    rows = blocks * BLOCK
    keys = [keys_of(r) for r in kv_refs]
    values = [values_of(r) for r in kv_refs]
    for c in range(len(middle)):
        kt[:, c * rows : (c + 1) * rows] = keys[c][...].T
    for i in range(blocks):
        span = slice(i * lanes, (i + 1) * lanes)
        s_i, g_i = s_ref.at[i % 2], g_ref.at[i % 2]
        top = score_pass(
            i, distances, blocks, reach, flag_ref, keys, values, qs[span, :], gs[span, :], s_i, g_i
        )
        before = m_ref[i : i + 1, :]
        top = jnp.maximum(top, before)
        base = top * SCALE_LOG2
        total, dot_total = weight_pass(i, distances, blocks, reach, flag_ref, s_i, g_i, base, True)
        fade = jnp.exp2(before * SCALE_LOG2 - base)
        total = total + l_ref[i : i + 1, :] * fade
        dot_total = dot_total + r_ref[i : i + 1, :] * fade
        inverse = 1.0 / total
        delta = dot_total * inverse
        stat_ref[0, i : i + 1, :] = base
        stat_ref[1, i : i + 1, :] = inverse
        stat_ref[2, i : i + 1, :] = delta
        gradients(i, middle, blocks, reach, lanes, s_i, g_i, p_ref, ds_ref, inverse, delta)
    for c, d in enumerate(middle):
        key_value_sums(c, d, blocks, reach, lanes, p_ref, ds_ref, qs, gs, out_refs[c])
    for i in range(blocks):
        if middle:
            part_ref[i] = query_sum(i, middle, blocks, reach, lanes, kt, ds_ref)
        else:
            part_ref[i] = jnp.zeros_like(part_ref[i])


def gradient_kernel(blocks, reach, heads, distances, final, flag_ref, qs, gs, stat_ref, part_ref, *refs):
    count = len(distances)
    keys, values = [], []
    for d in distances:
        if d == 0:
            keys.append(refs[0])
            values.append(refs[1])
            refs = refs[2:]
        else:
            keys.append(keys_of(refs[0]))
            values.append(values_of(refs[0]))
            refs = refs[1:]
    out_refs, query_out = refs[:count], refs[count]
    kt, s_ref, g_ref, p_ref, ds_ref = refs[count + 1 :]
    lanes = heads * BLOCK
    rows = blocks * BLOCK
    for c in range(count):
        kt[:, c * rows : (c + 1) * rows] = keys[c][...].T
    for i in range(blocks):
        span = slice(i * lanes, (i + 1) * lanes)
        s_i, g_i = s_ref.at[i % 2], g_ref.at[i % 2]
        score_pass(i, distances, blocks, reach, flag_ref, keys, values, qs[span, :], gs[span, :], s_i, g_i)
        weight_pass(i, distances, blocks, reach, flag_ref, s_i, g_i, stat_ref[0, i : i + 1, :], True)
        gradients(
            i, distances, blocks, reach, lanes, s_i, g_i, p_ref, ds_ref,
            stat_ref[1, i : i + 1, :], stat_ref[2, i : i + 1, :],
        )
    for c, d in enumerate(distances):
        key_value_sums(c, d, blocks, reach, lanes, p_ref, ds_ref, qs, gs, out_refs[c])
    for i in range(blocks):
        total = part_ref[i] + query_sum(i, distances, blocks, reach, lanes, kt, ds_ref)
        if not final:
            query_out[i] = total
            continue
        total = total * SCALE
        for h in range(heads):
            query_out[i * BLOCK : (i + 1) * BLOCK, h * HEAD_WIDTH : (h + 1) * HEAD_WIDTH] = (
                total[:, h * BLOCK : (h + 1) * BLOCK].T.astype(query_out.dtype)
            )


def kernel_call(kernel, flags, arrays, outs, scratch, weight=0, in_place=()):
    size = sum(a.size * a.dtype.itemsize for n, a in enumerate(arrays) if n not in in_place)
    size += sum(a.size * a.dtype.itemsize for a in outs)
    held = sum(math.prod(s.shape) * jnp.dtype(s.dtype).itemsize for s in scratch if hasattr(s, "dtype") and len(s.shape) > 1)
    return pl.pallas_call(
        kernel,
        out_shape=outs,
        in_specs=[pl.BlockSpec(memory_space=pltpu.SMEM)]
        + [pl.BlockSpec(memory_space=pl.ANY if n in in_place else pltpu.VMEM) for n in range(len(arrays))],
        out_specs=[pl.BlockSpec(memory_space=pltpu.VMEM)] * len(outs),
        scratch_shapes=scratch,
        compiler_params=pltpu.CompilerParams(vmem_limit_bytes=held + size + (8 << 20)),
        cost_estimate=pl.CostEstimate(flops=0, bytes_accessed=size * weight, transcendentals=0),
    )(flags, *arrays)


def attention_flags(doc_blocks, blocks, reach, place):
    query_ids = place * blocks + jnp.arange(blocks, dtype=jnp.int32)
    column = jnp.arange((reach + 1) * blocks, dtype=jnp.int32)
    key_ids = (place - column // blocks) * blocks + column % blocks
    behind = query_ids[:, None] - key_ids[None, :]
    listed = jnp.any(doc_blocks[:, :, None] == key_ids[None, None, :], axis=1)
    allowed = (key_ids[None, :] >= 0) & ((behind == 0) | (behind == 1) | ((behind >= 2) & listed))
    return allowed.astype(jnp.int32)


def pack_kernel(jobs, rows_ref, *refs):
    count = len(jobs)
    arrays, outs, sems = refs[: -count - 1], refs[-count - 1 : -1], refs[-1]
    copies = []
    for n, (members, size) in enumerate(jobs):
        start = pl.multiple_of(rows_ref[n], size)
        at = 0
        for member in members:
            array = arrays[member]
            width = array.shape[1]
            copies.append(
                pltpu.make_async_copy(
                    array.at[pl.ds(start, size), :], outs[n].at[:, at : at + width], sems.at[len(copies)]
                )
            )
            at += width
    for copy in copies:
        copy.start()
    for copy in copies:
        copy.wait()


def packed(jobs):
    arrays, plan = [], []
    for group, _, size in jobs:
        members = []
        for array in group:
            known = [n for n, a in enumerate(arrays) if a is array]
            if not known:
                arrays.append(array)
            members.append(known[0] if known else len(arrays) - 1)
        plan.append((tuple(members), size))
    starts = jnp.stack([jnp.asarray(start, jnp.int32) for _, start, _ in jobs])
    outs = [
        jax.ShapeDtypeStruct((size, sum(arrays[m].shape[1] for m in members)), arrays[0].dtype)
        for members, size in plan
    ]
    return pl.pallas_call(
        functools.partial(pack_kernel, plan),
        out_shape=outs,
        in_specs=[pl.BlockSpec(memory_space=pltpu.SMEM)] + [pl.BlockSpec(memory_space=pl.ANY)] * len(arrays),
        out_specs=[pl.BlockSpec(memory_space=pltpu.VMEM)] * len(outs),
        scratch_shapes=[pltpu.SemaphoreType.DMA((sum(len(members) for members, _ in plan),))],
        cost_estimate=pl.CostEstimate(
            flops=0, bytes_accessed=sum(2 * o.size * o.dtype.itemsize for o in outs), transcendentals=0
        ),
    )(starts, *arrays)


def product_kernel(peers, group_count, query_width, last, place_ref, *refs):
    before, refs = (refs[0], refs[1:]) if last else (None, refs)
    out_ref, left, right, acc, base, sems = refs[-6:]
    rows_out = right.shape[1]
    copies = []
    at = 0
    for n, (parts, low, high) in enumerate(peers):
        moves = []
        for piece, first in parts:
            width = refs[piece].shape[1]
            moves.append((refs[piece], left.at[n, :, first : first + width]))
        columns = slice(parts[0][1], parts[-1][1] + refs[parts[-1][0]].shape[1])
        weights = refs[low:high]
        share = rows_out // len(weights)
        for step, array in enumerate(weights):
            source = lax.rem(place_ref[0] - step + group_count, group_count) if len(weights) > 1 else 0
            span = pl.ds(pl.multiple_of(source * share, share), share)
            moves.append((array.at[:, columns], right.at[n, span, columns]))
        copies.append([pltpu.make_async_copy(a, b, sems.at[at + m]) for m, (a, b) in enumerate(moves)])
        at += len(moves)
    if last:
        copies[-1].append(pltpu.make_async_copy(before, base, sems.at[at]))
    for group in copies:
        for copy in group:
            copy.start()
    for n, (parts, _, _) in enumerate(peers):
        for copy in copies[n]:
            copy.wait()
        columns = slice(parts[0][1], parts[-1][1] + refs[parts[-1][0]].shape[1])
        for at in range(0, rows_out, rows_out // 4):
            span = slice(at, at + rows_out // 4)
            total = lax.dot_general(
                left[n, :, columns], right[n, span, columns], NT, preferred_element_type=jnp.float32
            )
            if n:
                total = total + acc[:, span]
            if last and n == len(peers) - 1:
                total = total + base[:, span].astype(jnp.float32)
            if n < len(peers) - 1:
                acc[:, span] = total
            else:
                out_ref[:, span] = total.astype(out_ref.dtype)


def body(query, key_head_rows, value_head_rows, output_gradient, doc_blocks, w_query, key_weight, value_weight):
    rows = query.shape[0]
    blocks = rows // BLOCK
    heads = query.shape[1] // key_head_rows.shape[1]
    lanes = heads * BLOCK
    reach = min(8, lax.axis_size("seq") - 1)
    place = lax.axis_index("seq")
    tp_count = lax.axis_size("tp")
    tp_place = lax.axis_index("tp")
    group_count = lax.axis_size("groups")
    group_place = lax.axis_index("groups")
    rows_out = w_query.shape[0] // tp_count
    share = rows_out // group_count
    bf16, f32 = jnp.bfloat16, jnp.float32

    weights = (w_query, key_weight, value_weight)
    own_kv = (key_head_rows, value_head_rows)

    def share_of(bits):
        return ((tp_place ^ bits) * rows_out + group_place * share, share)

    early = range(2, min(3, tp_count))
    late = range(3, tp_count)
    with jax.named_scope("pack_first"):
        key_value, *sent = packed([(own_kv, 0, rows)] + [(weights, *share_of(bits)) for bits in early])
    with jax.named_scope("kv_forward"):
        window = {1: shifted(key_value, "seq", 1)}
        if reach > 1:
            window[reach] = shifted(key_value, "seq", reach)
        for d in range(2, reach):
            window[d] = shifted(window[d - 1], "seq", 1)
        far = tuple(range(2, reach + 1))
    with jax.named_scope("pack_rest"):
        held, _ = lax.optimization_barrier((weights, key_value))
        pair_weights, own_weights, *more = packed(
            [(held, (tp_place ^ 1) * rows_out, rows_out), (held, tp_place * rows_out, rows_out)]
            + [(held, *share_of(bits)) for bits in late]
        )
    with jax.named_scope("weight_exchange"):
        whole = [own_weights, swapped(pair_weights, "tp", 1)]
        sent = [swapped(piece, "tp", bits) for bits, piece in zip([*early, *late], sent + more)]

    with jax.named_scope("flags"):
        flags = attention_flags(doc_blocks, blocks, reach, place)

    def scratch(count, gradient_count):
        tiles = [pltpu.VMEM((2, count * rows, lanes), f32)] * 2
        if not gradient_count:
            return tiles
        turned = [pltpu.VMEM((HEAD_WIDTH, gradient_count * rows), bf16)]
        return turned + tiles + [pltpu.VMEM((gradient_count * rows, blocks * lanes), bf16)] * 2

    near_in = [query, output_gradient, key_head_rows, value_head_rows, window[1]]
    stats = [jax.ShapeDtypeStruct((blocks, lanes), f32)] * 3
    stats += [jax.ShapeDtypeStruct((blocks * lanes, HEAD_WIDTH), bf16)] * 2
    near_in[0], pair_weights = lax.optimization_barrier((near_in[0], pair_weights))
    with jax.named_scope("near_stats"):
        top, total, dot_total, query_stack, grad_stack = kernel_call(
            functools.partial(near_stats_kernel, blocks, reach, heads),
            flags, near_in, stats, scratch(2, 0),
        )
    grads = {}
    kv_shape = (rows, 2 * HEAD_WIDTH)
    part_shape = jax.ShapeDtypeStruct((blocks, HEAD_WIDTH, lanes), f32)
    if far:
        middle = far[:-1]
        with jax.named_scope("far_stats"):
            stat, part, *middle_grads = kernel_call(
                functools.partial(far_kernel, blocks, reach, heads, far, middle),
                flags,
                [query_stack, grad_stack, top, total, dot_total] + [window[d] for d in far],
                [jax.ShapeDtypeStruct((3, blocks, lanes), f32), part_shape]
                + [jax.ShapeDtypeStruct(kv_shape, bf16)] * len(middle),
                scratch(len(far), max(len(middle), 1)),
            )
        grads = dict(zip(middle, middle_grads))
        with jax.named_scope("longest_gradients"):
            grads[reach], part = kernel_call(
                functools.partial(gradient_kernel, blocks, reach, heads, (reach,), False),
                flags,
                [query_stack, grad_stack, stat, part, window[reach]],
                [jax.ShapeDtypeStruct(kv_shape, bf16), part_shape],
                scratch(1, 1),
            )
    else:
        stat = jnp.stack([top * SCALE_LOG2, 1.0 / total, dot_total / total])
        part = jnp.zeros(part_shape.shape, f32)
    def passed_on(piece, after):
        held, _ = lax.optimization_barrier((piece, after))
        moved = [piece]
        for step in range(1, group_count):
            route = [(i, (i + step) % group_count) for i in range(group_count)]
            moved.append(lax.ppermute(held, "groups", route))
        return moved

    with jax.named_scope("weight_exchange"):
        shares = passed_on(sent[0], stat) if sent else []

    with jax.named_scope("near_gradients"):
        own, grads[1], query_grad = kernel_call(
            functools.partial(gradient_kernel, blocks, reach, heads, (0, 1), True),
            flags,
            [query_stack, grad_stack, stat, part, key_head_rows, value_head_rows, window[1]],
            [
                jax.ShapeDtypeStruct(kv_shape, f32),
                jax.ShapeDtypeStruct(kv_shape, f32),
                jax.ShapeDtypeStruct(query.shape, bf16),
            ],
            scratch(2, 2),
        )

    with jax.named_scope("weight_exchange"):
        for piece in sent[1:]:
            shares += passed_on(piece, query_grad)
    with jax.named_scope("kv_return"):
        if far:
            longest = shifted(grads[reach], "seq", -reach)
            passed = None
            for d in range(reach - 1, 0, -1):
                total = grads[d] if passed is None else (grads[d].astype(f32) + passed.astype(f32))
                total = total.astype(bf16)
                passed = shifted(total, "seq", -1)
        else:
            passed = shifted(grads[1].astype(bf16), "seq", -1)
        if far:
            longest, passed, *shares[1:2] = lax.optimization_barrier((longest, passed, *shares[1:2]))
            own = own + longest.astype(f32)
        key_value_grad = (own + passed.astype(f32)).astype(bf16)

    def gathered(block, before_last=None):
        pieces = [block, swapped(block, "tp", 1)]
        for bits in range(2, tp_count, 2):
            pieces.append(swapped(block, "tp", bits))
            held = pieces[-1]
            if before_last is not None:
                held, _ = lax.optimization_barrier((held, before_last))
            pieces.append(swapped(held, "tp", 1))
        return pieces

    with jax.named_scope("query_grad_gather"):
        q_pieces = gathered(query_grad)
    width = query.shape[1]
    total_width = width + 2 * HEAD_WIDTH
    place_ids = jnp.full((1,), group_place, jnp.int32)

    def product(scope, before, entries, out_type):
        arrays = [] if before is None else [before]
        peers = []
        for parts, weights in entries:
            placed = []
            for piece, first in parts:
                placed.append((len(arrays) - (before is not None), first))
                arrays.append(piece)
            low = len(arrays) - (before is not None)
            arrays += weights
            peers.append((tuple(placed), low, low + len(weights)))
        count = sum(len(parts) + len(weights) for parts, weights in entries) + 1
        with jax.named_scope(scope):
            (result,) = kernel_call(
                functools.partial(product_kernel, peers, group_count, width, before is not None),
                place_ids,
                arrays,
                [jax.ShapeDtypeStruct((rows, rows_out), out_type)],
                [
                    pltpu.VMEM((len(entries), rows, total_width), bf16),
                    pltpu.VMEM((len(entries), rows_out, total_width), bf16),
                    pltpu.VMEM((rows, rows_out), f32),
                    pltpu.VMEM((rows, rows_out), f32 if before is None else before.dtype),
                    pltpu.SemaphoreType.DMA((count,)),
                ],
                1,
                range(len(arrays)),
            )
        return result

    sets = [[whole[0]], [whole[1]]]
    sets += [shares[at : at + group_count] for at in range(0, len(shares), group_count)]
    acc = product(
        "query_product", None, [([(q_pieces[bits], 0)], sets[bits]) for bits in range(tp_count - 1)], f32
    )
    with jax.named_scope("kv_grad_gather"):
        kv_pieces = gathered(key_value_grad, [acc] + shares[-1:])
    entries = [([(kv_pieces[bits], width)], sets[bits]) for bits in range(tp_count - 1)]
    entries.append(([(q_pieces[-1], 0), (kv_pieces[-1], width)], sets[-1]))
    return product("last_product", acc, entries, bf16)


def solution(mesh):
    in_specs = (
        P(("groups", "seq"), "tp"),
        P(("groups", "seq"), "tp"),
        P(("groups", "seq"), "tp"),
        P(("groups", "seq"), "tp"),
        P(("groups", "seq"), None),
        P(None, "tp"),
        P(None, "tp"),
        P(None, "tp"),
    )
    out_specs = P(("groups", "seq"), "tp")
    return jax.shard_map(body, mesh=mesh, in_specs=in_specs, out_specs=out_specs, check_vma=False)
```

```python
import functools
import math

import jax
import jax.numpy as jnp
from jax import lax
from jax.experimental import pallas as pl
from jax.experimental.pallas import tpu as pltpu
from jax.sharding import PartitionSpec as P

HEAD_WIDTH = 128
BLOCK = 128
SCALE = HEAD_WIDTH ** (-0.5)
SCALE_LOG2 = SCALE * 1.4426950408889634
LOWEST = -1e30
NT = (((1,), (1,)), ((), ()))


def shifted(block, axis, distance):
    devices = range(lax.axis_size(axis))
    route = [(i - distance, i) for i in devices if i - distance in devices]
    return lax.ppermute(block, axis, route)


def swapped(block, axis, bits):
    return lax.ppermute(block, axis, [(i, i ^ bits) for i in range(lax.axis_size(axis))])


def key_range(distance, i, blocks, reach):
    if distance == 0:
        return 0, i + 1
    if distance == reach:
        return i, blocks
    return 0, blocks


def lane_range(distance, j, blocks, reach):
    if distance == 0:
        return j, blocks
    if distance == reach:
        return 0, j + 1
    return 0, blocks


def stack_heads(rows_ref, stack_ref, blocks, heads):
    for i in range(blocks):
        for h in range(heads):
            at = (i * heads + h) * BLOCK
            stack_ref[at : at + BLOCK, :] = rows_ref[
                i * BLOCK : (i + 1) * BLOCK, h * HEAD_WIDTH : (h + 1) * HEAD_WIDTH
            ]


def band_keep(offset, lanes):
    key_at = lax.broadcasted_iota(jnp.int32, (BLOCK, lanes), 0)
    query_at = lax.broadcasted_iota(jnp.int32, (BLOCK, lanes), 1) % BLOCK
    return key_at <= query_at if offset == 0 else key_at > query_at


def fold(tile, op):
    rows = tile.shape[0]
    total = tile[0:8]
    for at in range(8, rows, 8):
        total = op(total, tile[at : at + 8])
    return total


def keys_of(ref):
    return ref.at[:, 0:HEAD_WIDTH]


def values_of(ref):
    return ref.at[:, HEAD_WIDTH : 2 * HEAD_WIDTH]


def tiles_of(distances, i, blocks, reach):
    return [
        (c, d, j)
        for c, d in enumerate(distances)
        for j in range(*key_range(d, i, blocks, reach))
    ]


def score_pass(i, distances, blocks, reach, flag_ref, key_refs, value_refs, query_i, grad_i, s_ref, g_ref):
    rows = blocks * BLOCK
    top = None
    for c, d in enumerate(distances):
        low, high = key_range(d, i, blocks, reach)
        span = slice(low * BLOCK, high * BLOCK)
        at = slice(c * rows + low * BLOCK, c * rows + high * BLOCK)
        s_ref[at, :] = lax.dot_general(key_refs[c][span, :], query_i, NT, preferred_element_type=jnp.float32)
        g_ref[at, :] = lax.dot_general(value_refs[c][span, :], grad_i, NT, preferred_element_type=jnp.float32)
    for c, d, j in tiles_of(distances, i, blocks, reach):
        at = slice(c * rows + j * BLOCK, c * rows + (j + 1) * BLOCK)
        offset = d * blocks + i - j
        tile = s_ref[at, :]
        if offset < 2:
            tile = jnp.where(band_keep(offset, tile.shape[1]), tile, LOWEST)
            s_ref[at, :] = tile
        part = fold(tile, jnp.maximum)
        if offset > 0:
            part = jnp.where(flag_ref[i, d * blocks + j] != 0, part, LOWEST)
        top = part if top is None else jnp.maximum(top, part)
    return jnp.max(top, axis=0, keepdims=True)


def shift_of(flag_ref, i, d, j, blocks, base):
    if d * blocks + i - j == 0:
        return base
    return jnp.where(flag_ref[i, d * blocks + j] != 0, base, -LOWEST)


def weight_pass(i, distances, blocks, reach, flag_ref, s_ref, g_ref, base, keep):
    rows = blocks * BLOCK
    total = dot_total = None
    for c, d, j in tiles_of(distances, i, blocks, reach):
        at = slice(c * rows + j * BLOCK, c * rows + (j + 1) * BLOCK)
        weights = jnp.exp2(s_ref[at, :] * SCALE_LOG2 - shift_of(flag_ref, i, d, j, blocks, base))
        if keep:
            s_ref[at, :] = weights
        part = fold(weights, jnp.add)
        dot_part = fold(weights * g_ref[at, :], jnp.add)
        total = part if total is None else total + part
        dot_total = dot_part if dot_total is None else dot_total + dot_part
    return jnp.sum(total, axis=0, keepdims=True), jnp.sum(dot_total, axis=0, keepdims=True)


def key_value_sums(c, d, blocks, reach, lanes, p_ref, ds_ref, query_stack, grad_stack, out_ref):
    rows = blocks * BLOCK
    ranges = [lane_range(d, j, blocks, reach) for j in range(blocks)]
    whole = all(r == (0, blocks) for r in ranges)
    for j, (low, high) in enumerate(ranges[:1] if whole else ranges):
        out = slice(j * BLOCK, rows if whole else (j + 1) * BLOCK)
        at = slice(c * rows + out.start, c * rows + out.stop)
        span = slice(low * lanes, high * lanes)
        key_sum = jnp.dot(ds_ref[at, span], query_stack[span, :], preferred_element_type=jnp.float32)
        out_ref[out, 0:HEAD_WIDTH] = (key_sum * SCALE).astype(out_ref.dtype)
        value_sum = jnp.dot(p_ref[at, span], grad_stack[span, :], preferred_element_type=jnp.float32)
        out_ref[out, HEAD_WIDTH:] = value_sum.astype(out_ref.dtype)


def query_sum(i, distances, blocks, reach, lanes, key_turned, ds_ref):
    rows = blocks * BLOCK
    total = None
    for c, d in enumerate(distances):
        low, high = key_range(d, i, blocks, reach)
        at = slice(c * rows + low * BLOCK, c * rows + high * BLOCK)
        part = jnp.dot(
            key_turned[:, at], ds_ref[at, i * lanes : (i + 1) * lanes], preferred_element_type=jnp.float32
        )
        total = part if total is None else total + part
    return total


def near_stats_kernel(blocks, reach, heads, flag_ref, query_ref, grad_ref, k0, v0, kv1, m_ref, l_ref, r_ref, qs, gs, s_ref, g_ref):
    lanes = heads * BLOCK
    stack_heads(query_ref, qs, blocks, heads)
    stack_heads(grad_ref, gs, blocks, heads)
    for i in range(blocks):
        span = slice(i * lanes, (i + 1) * lanes)
        s_i, g_i = s_ref.at[i % 2], g_ref.at[i % 2]
        top = score_pass(
            i, (0, 1), blocks, reach, flag_ref, (k0, keys_of(kv1)), (v0, values_of(kv1)), qs[span, :], gs[span, :], s_i, g_i
        )
        total, dot_total = weight_pass(
            i, (0, 1), blocks, reach, flag_ref, s_i, g_i, top * SCALE_LOG2, False
        )
        m_ref[i : i + 1, :] = top
        l_ref[i : i + 1, :] = total
        r_ref[i : i + 1, :] = dot_total


def gradients(i, distances, blocks, reach, lanes, s_i, g_i, p_ref, ds_ref, inverse, delta):
    rows = blocks * BLOCK
    span = slice(i * lanes, (i + 1) * lanes)
    for c, d, j in tiles_of(distances, i, blocks, reach):
        at = slice(c * rows + j * BLOCK, c * rows + (j + 1) * BLOCK)
        probability = s_i[at, :] * inverse
        p_ref[at, span] = probability.astype(jnp.bfloat16)
        ds_ref[at, span] = (probability * (g_i[at, :] - delta)).astype(jnp.bfloat16)


def far_kernel(blocks, reach, heads, distances, middle, *refs):
    count = len(distances)
    flag_ref, qs, gs, m_ref, l_ref, r_ref = refs[:6]
    kv_refs = refs[6 : 6 + count]
    stat_ref, part_ref = refs[6 + count : 8 + count]
    out_refs = refs[8 + count : 8 + count + len(middle)]
    kt, s_ref, g_ref, p_ref, ds_ref = refs[8 + count + len(middle) :]
    lanes = heads * BLOCK
    rows = blocks * BLOCK
    keys = [keys_of(r) for r in kv_refs]
    values = [values_of(r) for r in kv_refs]
    for c in range(len(middle)):
        kt[:, c * rows : (c + 1) * rows] = keys[c][...].T
    for i in range(blocks):
        span = slice(i * lanes, (i + 1) * lanes)
        s_i, g_i = s_ref.at[i % 2], g_ref.at[i % 2]
        top = score_pass(
            i, distances, blocks, reach, flag_ref, keys, values, qs[span, :], gs[span, :], s_i, g_i
        )
        before = m_ref[i : i + 1, :]
        top = jnp.maximum(top, before)
        base = top * SCALE_LOG2
        total, dot_total = weight_pass(i, distances, blocks, reach, flag_ref, s_i, g_i, base, True)
        fade = jnp.exp2(before * SCALE_LOG2 - base)
        total = total + l_ref[i : i + 1, :] * fade
        dot_total = dot_total + r_ref[i : i + 1, :] * fade
        inverse = 1.0 / total
        delta = dot_total * inverse
        stat_ref[0, i : i + 1, :] = base
        stat_ref[1, i : i + 1, :] = inverse
        stat_ref[2, i : i + 1, :] = delta
        gradients(i, middle, blocks, reach, lanes, s_i, g_i, p_ref, ds_ref, inverse, delta)
    for c, d in enumerate(middle):
        key_value_sums(c, d, blocks, reach, lanes, p_ref, ds_ref, qs, gs, out_refs[c])
    for i in range(blocks):
        if middle:
            part_ref[i] = query_sum(i, middle, blocks, reach, lanes, kt, ds_ref)
        else:
            part_ref[i] = jnp.zeros_like(part_ref[i])


def gradient_kernel(blocks, reach, heads, distances, final, flag_ref, qs, gs, stat_ref, part_ref, *refs):
    count = len(distances)
    keys, values = [], []
    for d in distances:
        if d == 0:
            keys.append(refs[0])
            values.append(refs[1])
            refs = refs[2:]
        else:
            keys.append(keys_of(refs[0]))
            values.append(values_of(refs[0]))
            refs = refs[1:]
    out_refs, query_out = refs[:count], refs[count]
    kt, s_ref, g_ref, p_ref, ds_ref = refs[count + 1 :]
    lanes = heads * BLOCK
    rows = blocks * BLOCK
    for c in range(count):
        kt[:, c * rows : (c + 1) * rows] = keys[c][...].T
    for i in range(blocks):
        span = slice(i * lanes, (i + 1) * lanes)
        s_i, g_i = s_ref.at[i % 2], g_ref.at[i % 2]
        score_pass(i, distances, blocks, reach, flag_ref, keys, values, qs[span, :], gs[span, :], s_i, g_i)
        weight_pass(i, distances, blocks, reach, flag_ref, s_i, g_i, stat_ref[0, i : i + 1, :], True)
        gradients(
            i, distances, blocks, reach, lanes, s_i, g_i, p_ref, ds_ref,
            stat_ref[1, i : i + 1, :], stat_ref[2, i : i + 1, :],
        )
    for c, d in enumerate(distances):
        key_value_sums(c, d, blocks, reach, lanes, p_ref, ds_ref, qs, gs, out_refs[c])
    for i in range(blocks):
        total = part_ref[i] + query_sum(i, distances, blocks, reach, lanes, kt, ds_ref)
        if not final:
            query_out[i] = total
            continue
        total = total * SCALE
        for h in range(heads):
            query_out[i * BLOCK : (i + 1) * BLOCK, h * HEAD_WIDTH : (h + 1) * HEAD_WIDTH] = (
                total[:, h * BLOCK : (h + 1) * BLOCK].T.astype(query_out.dtype)
            )


def kernel_call(kernel, flags, arrays, outs, scratch, weight=0, in_place=()):
    size = sum(a.size * a.dtype.itemsize for n, a in enumerate(arrays) if n not in in_place)
    size += sum(a.size * a.dtype.itemsize for a in outs)
    held = sum(math.prod(s.shape) * jnp.dtype(s.dtype).itemsize for s in scratch if hasattr(s, "dtype") and len(s.shape) > 1)
    return pl.pallas_call(
        kernel,
        out_shape=outs,
        in_specs=[pl.BlockSpec(memory_space=pltpu.SMEM)]
        + [pl.BlockSpec(memory_space=pl.ANY if n in in_place else pltpu.VMEM) for n in range(len(arrays))],
        out_specs=[pl.BlockSpec(memory_space=pltpu.VMEM)] * len(outs),
        scratch_shapes=scratch,
        compiler_params=pltpu.CompilerParams(vmem_limit_bytes=held + size + (8 << 20)),
        cost_estimate=pl.CostEstimate(flops=0, bytes_accessed=size * weight, transcendentals=0),
    )(flags, *arrays)


def attention_flags(doc_blocks, blocks, reach, place):
    query_ids = place * blocks + jnp.arange(blocks, dtype=jnp.int32)
    column = jnp.arange((reach + 1) * blocks, dtype=jnp.int32)
    key_ids = (place - column // blocks) * blocks + column % blocks
    behind = query_ids[:, None] - key_ids[None, :]
    listed = jnp.any(doc_blocks[:, :, None] == key_ids[None, None, :], axis=1)
    allowed = (key_ids[None, :] >= 0) & ((behind == 0) | (behind == 1) | ((behind >= 2) & listed))
    return allowed.astype(jnp.int32)


def pack_kernel(jobs, rows_ref, *refs):
    count = len(jobs)
    arrays, outs, sems = refs[: -count - 1], refs[-count - 1 : -1], refs[-1]
    copies = []
    for n, (members, size) in enumerate(jobs):
        start = pl.multiple_of(rows_ref[n], size)
        at = 0
        for member in members:
            array = arrays[member]
            width = array.shape[1]
            copies.append(
                pltpu.make_async_copy(
                    array.at[pl.ds(start, size), :], outs[n].at[:, at : at + width], sems.at[len(copies)]
                )
            )
            at += width
    for copy in copies:
        copy.start()
    for copy in copies:
        copy.wait()


def packed(jobs):
    arrays, plan = [], []
    for group, _, size in jobs:
        members = []
        for array in group:
            known = [n for n, a in enumerate(arrays) if a is array]
            if not known:
                arrays.append(array)
            members.append(known[0] if known else len(arrays) - 1)
        plan.append((tuple(members), size))
    starts = jnp.stack([jnp.asarray(start, jnp.int32) for _, start, _ in jobs])
    outs = [
        jax.ShapeDtypeStruct((size, sum(arrays[m].shape[1] for m in members)), arrays[0].dtype)
        for members, size in plan
    ]
    return pl.pallas_call(
        functools.partial(pack_kernel, plan),
        out_shape=outs,
        in_specs=[pl.BlockSpec(memory_space=pltpu.SMEM)] + [pl.BlockSpec(memory_space=pl.ANY)] * len(arrays),
        out_specs=[pl.BlockSpec(memory_space=pltpu.VMEM)] * len(outs),
        scratch_shapes=[pltpu.SemaphoreType.DMA((sum(len(members) for members, _ in plan),))],
        cost_estimate=pl.CostEstimate(
            flops=0, bytes_accessed=sum(2 * o.size * o.dtype.itemsize for o in outs), transcendentals=0
        ),
    )(starts, *arrays)


def product_kernel(peers, group_count, query_width, last, place_ref, *refs):
    before, refs = (refs[0], refs[1:]) if last else (None, refs)
    out_ref, left, right, acc, base, sems = refs[-6:]
    rows_out = right.shape[1]
    copies = []
    at = 0
    for n, (parts, low, high) in enumerate(peers):
        moves = []
        for piece, first in parts:
            width = refs[piece].shape[1]
            moves.append((refs[piece], left.at[n, :, first : first + width]))
        columns = slice(parts[0][1], parts[-1][1] + refs[parts[-1][0]].shape[1])
        weights = refs[low:high]
        share = rows_out // len(weights)
        if n == 0:
            start, column = pl.multiple_of(place_ref[1] * rows_out, rows_out), columns.start
            for array in weights:
                width = array.shape[1]
                moves.append((array.at[pl.ds(start, rows_out), :], right.at[n, :, column : column + width]))
                column += width
            weights = ()
        for step, array in enumerate(weights):
            source = lax.rem(place_ref[0] - step + group_count, group_count) if len(weights) > 1 else 0
            span = pl.ds(pl.multiple_of(source * share, share), share)
            moves.append((array.at[:, columns], right.at[n, span, columns]))
        copies.append([pltpu.make_async_copy(a, b, sems.at[at + m]) for m, (a, b) in enumerate(moves)])
        at += len(moves)
    if last:
        copies[-1].append(pltpu.make_async_copy(before, base, sems.at[at]))
    for group in copies:
        for copy in group:
            copy.start()
    for n, (parts, _, _) in enumerate(peers):
        for copy in copies[n]:
            copy.wait()
        columns = slice(parts[0][1], parts[-1][1] + refs[parts[-1][0]].shape[1])
        for at in range(0, rows_out, rows_out // 4):
            span = slice(at, at + rows_out // 4)
            total = lax.dot_general(
                left[n, :, columns], right[n, span, columns], NT, preferred_element_type=jnp.float32
            )
            if n:
                total = total + acc[:, span]
            if last and n == len(peers) - 1:
                total = total + base[:, span].astype(jnp.float32)
            if n < len(peers) - 1:
                acc[:, span] = total
            else:
                out_ref[:, span] = total.astype(out_ref.dtype)


def body(query, key_head_rows, value_head_rows, output_gradient, doc_blocks, w_query, key_weight, value_weight):
    rows = query.shape[0]
    blocks = rows // BLOCK
    heads = query.shape[1] // key_head_rows.shape[1]
    lanes = heads * BLOCK
    reach = min(8, lax.axis_size("seq") - 1)
    place = lax.axis_index("seq")
    tp_count = lax.axis_size("tp")
    tp_place = lax.axis_index("tp")
    group_count = lax.axis_size("groups")
    group_place = lax.axis_index("groups")
    rows_out = w_query.shape[0] // tp_count
    share = rows_out // group_count
    bf16, f32 = jnp.bfloat16, jnp.float32

    weights = (w_query, key_weight, value_weight)
    own_kv = (key_head_rows, value_head_rows)

    def share_of(bits):
        return ((tp_place ^ bits) * rows_out + group_place * share, share)

    early = range(2, min(3, tp_count))
    late = range(3, tp_count)
    with jax.named_scope("pack_first"):
        key_value, *sent = packed([(own_kv, 0, rows)] + [(weights, *share_of(bits)) for bits in early])
    with jax.named_scope("kv_forward"):
        window = {1: shifted(key_value, "seq", 1)}
        if reach > 1:
            window[reach] = shifted(key_value, "seq", reach)
        for d in range(2, reach):
            window[d] = shifted(window[d - 1], "seq", 1)
        far = tuple(range(2, reach + 1))
    with jax.named_scope("pack_rest"):
        held, _ = lax.optimization_barrier((weights, key_value))
        pair_weights, *more = packed(
            [(held, (tp_place ^ 1) * rows_out, rows_out)]
            + [(held, *share_of(bits)) for bits in late]
        )
    with jax.named_scope("weight_exchange"):
        pair = swapped(pair_weights, "tp", 1)
        sent = [swapped(piece, "tp", bits) for bits, piece in zip([*early, *late], sent + more)]

    with jax.named_scope("flags"):
        flags = attention_flags(doc_blocks, blocks, reach, place)

    def scratch(count, gradient_count):
        tiles = [pltpu.VMEM((2, count * rows, lanes), f32)] * 2
        if not gradient_count:
            return tiles
        turned = [pltpu.VMEM((HEAD_WIDTH, gradient_count * rows), bf16)]
        return turned + tiles + [pltpu.VMEM((gradient_count * rows, blocks * lanes), bf16)] * 2

    near_in = [query, output_gradient, key_head_rows, value_head_rows, window[1]]
    stats = [jax.ShapeDtypeStruct((blocks, lanes), f32)] * 3
    stats += [jax.ShapeDtypeStruct((blocks * lanes, HEAD_WIDTH), bf16)] * 2
    near_in[0], pair_weights = lax.optimization_barrier((near_in[0], pair_weights))
    with jax.named_scope("near_stats"):
        top, total, dot_total, query_stack, grad_stack = kernel_call(
            functools.partial(near_stats_kernel, blocks, reach, heads),
            flags, near_in, stats, scratch(2, 0),
        )
    grads = {}
    kv_shape = (rows, 2 * HEAD_WIDTH)
    part_shape = jax.ShapeDtypeStruct((blocks, HEAD_WIDTH, lanes), f32)
    if far:
        middle = far[:-1]
        with jax.named_scope("far_stats"):
            stat, part, *middle_grads = kernel_call(
                functools.partial(far_kernel, blocks, reach, heads, far, middle),
                flags,
                [query_stack, grad_stack, top, total, dot_total] + [window[d] for d in far],
                [jax.ShapeDtypeStruct((3, blocks, lanes), f32), part_shape]
                + [jax.ShapeDtypeStruct(kv_shape, bf16)] * len(middle),
                scratch(len(far), max(len(middle), 1)),
            )
        grads = dict(zip(middle, middle_grads))
        with jax.named_scope("longest_gradients"):
            grads[reach], part = kernel_call(
                functools.partial(gradient_kernel, blocks, reach, heads, (reach,), False),
                flags,
                [query_stack, grad_stack, stat, part, window[reach]],
                [jax.ShapeDtypeStruct(kv_shape, bf16), part_shape],
                scratch(1, 1),
            )
    else:
        stat = jnp.stack([top * SCALE_LOG2, 1.0 / total, dot_total / total])
        part = jnp.zeros(part_shape.shape, f32)
    def passed_on(piece, after):
        held, _ = lax.optimization_barrier((piece, after))
        moved = [piece]
        for step in range(1, group_count):
            route = [(i, (i + step) % group_count) for i in range(group_count)]
            moved.append(lax.ppermute(held, "groups", route))
        return moved

    with jax.named_scope("weight_exchange"):
        shares = passed_on(sent[0], stat) if sent else []

    with jax.named_scope("near_gradients"):
        own, grads[1], query_grad = kernel_call(
            functools.partial(gradient_kernel, blocks, reach, heads, (0, 1), True),
            flags,
            [query_stack, grad_stack, stat, part, key_head_rows, value_head_rows, window[1]],
            [
                jax.ShapeDtypeStruct(kv_shape, f32),
                jax.ShapeDtypeStruct(kv_shape, f32),
                jax.ShapeDtypeStruct(query.shape, bf16),
            ],
            scratch(2, 2),
        )

    with jax.named_scope("weight_exchange"):
        for piece in sent[1:]:
            shares += passed_on(piece, query_grad)
    with jax.named_scope("kv_return"):
        if far:
            longest = shifted(grads[reach], "seq", -reach)
            passed = None
            for d in range(reach - 1, 0, -1):
                total = grads[d] if passed is None else (grads[d].astype(f32) + passed.astype(f32))
                total = total.astype(bf16)
                passed = shifted(total, "seq", -1)
        else:
            passed = shifted(grads[1].astype(bf16), "seq", -1)
        if far:
            longest, passed, *shares[1:2] = lax.optimization_barrier((longest, passed, *shares[1:2]))
            own = own + longest.astype(f32)
        key_value_grad = (own + passed.astype(f32)).astype(bf16)

    def gathered(block, before_last=None):
        pieces = [block, swapped(block, "tp", 1)]
        for bits in range(2, tp_count, 2):
            pieces.append(swapped(block, "tp", bits))
            held = pieces[-1]
            if before_last is not None:
                held, _ = lax.optimization_barrier((held, before_last))
            pieces.append(swapped(held, "tp", 1))
        return pieces

    with jax.named_scope("query_grad_gather"):
        q_pieces = gathered(query_grad)
    width = query.shape[1]
    total_width = width + 2 * HEAD_WIDTH
    place_ids = jnp.stack([group_place, tp_place]).astype(jnp.int32)

    def product(scope, before, entries, out_type):
        arrays = [] if before is None else [before]
        peers = []
        for parts, weights in entries:
            placed = []
            for piece, first in parts:
                placed.append((len(arrays) - (before is not None), first))
                arrays.append(piece)
            low = len(arrays) - (before is not None)
            arrays += weights
            peers.append((tuple(placed), low, low + len(weights)))
        count = sum(len(parts) + len(weights) for parts, weights in entries) + 1
        with jax.named_scope(scope):
            (result,) = kernel_call(
                functools.partial(product_kernel, peers, group_count, width, before is not None),
                place_ids,
                arrays,
                [jax.ShapeDtypeStruct((rows, rows_out), out_type)],
                [
                    pltpu.VMEM((len(entries), rows, total_width), bf16),
                    pltpu.VMEM((len(entries), rows_out, total_width), bf16),
                    pltpu.VMEM((rows, rows_out), f32),
                    pltpu.VMEM((rows, rows_out), f32 if before is None else before.dtype),
                    pltpu.SemaphoreType.DMA((count,)),
                ],
                1,
                range(len(arrays)),
            )
        return result

    sets = [[w_query], [pair]]
    sets += [shares[at : at + group_count] for at in range(0, len(shares), group_count)]
    acc = product(
        "query_product", None, [([(q_pieces[bits], 0)], sets[bits]) for bits in range(tp_count - 1)], f32
    )
    with jax.named_scope("kv_grad_gather"):
        kv_pieces = gathered(key_value_grad, [acc] + shares[-1:])
    sets[0] = [key_weight, value_weight]
    entries = [([(kv_pieces[bits], width)], sets[bits]) for bits in range(tp_count - 1)]
    entries.append(([(q_pieces[-1], 0), (kv_pieces[-1], width)], sets[-1]))
    return product("last_product", acc, entries, bf16)


def solution(mesh):
    in_specs = (
        P(("groups", "seq"), "tp"),
        P(("groups", "seq"), "tp"),
        P(("groups", "seq"), "tp"),
        P(("groups", "seq"), "tp"),
        P(("groups", "seq"), None),
        P(None, "tp"),
        P(None, "tp"),
        P(None, "tp"),
    )
    out_specs = P(("groups", "seq"), "tp")
    return jax.shard_map(body, mesh=mesh, in_specs=in_specs, out_specs=out_specs, check_vma=False)
```
